32 devices in a mesh: groups: 2 (over y), stn: 4 (over z), hour: 2 (over x), freq: 2 (over core).
Axes of the slice: x: 2, y: 2, z: 4, core: 2. Of those that a mesh axis runs over, the one named last changes fastest.
Arguments:
- spectra: bfloat16 [32, 512, 2, 512], P(('groups', 'hour'), 'stn', None, 'freq'), parts along dimension 0, may hold values from -6 to 6
- uptime: int32 [32, 512], P(('groups', 'hour'), 'stn'), parts along dimension 0, may hold values 0 or 1
- pair_blocks: int32 [16, 2], P('groups'), parts along dimension 0, may hold values from 0 to 63, as said below
Outputs:
- correlations: float32 [1024, 1024], P(('groups', 'stn', 'hour', 'freq')), parts along dimension 0
The draws below stay inside these ranges and needn't reach their ends.
There are 2 independent parts, one for each index of `groups`. The reference program is written for one: setup_inputs(seed, part) draws one part's arguments, and reference() takes and returns one part's arrays. A program takes and returns all parts, laid end to end along the dimension named above; each array names one. Nothing has to cross between parts.
Inputs may be any that keep to these rules, and one draw needn't show every extreme that they name: `pair_blocks`: rows r * 2 to (r + 1) * 2 - 1 are the pair blocks read by station row r. Within one reader's rows all 4 block numbers differ; at most 2 of them lie among one owner's blocks (o * 16 to (o + 1) * 16 - 1), and for some owner exactly 2 do.
All inputs are finite; a program needn't handle non-finite values. No bound on the sum of `uptime` on one device may be relied on, other than what follows from the above.
Results may differ from the reference program's by a relative error of at most 0.0003.
Values may be sent and summed in bfloat16 or wider, within the bound.
No kernel may reach another device: no remote copies, remote signals or barrier semaphores. Data moves between devices by JAX's collectives and lax.ppermute only.
A program may use at most 128 MiB of HBM per device.

```python
import math
import jax
import jax.numpy as jnp
from jax import lax

L = 1024
F = 512
SB = 8
CAP = 2
STATIONS = 512
HOURS = 16
BO = 16
NB = 64
PB = 2
PAIRS = 512
N_STN = 4


def draw_pair_blocks(key, part):
    key = jax.random.fold_in(key, 7)
    tickets = N_STN * CAP
    owners = jnp.arange(tickets, dtype=jnp.int32) // CAP
    within = jnp.arange(tickets, dtype=jnp.int32) % CAP

    def one_reader(reader_key):
        keys = jax.random.split(reader_key, 4)
        forced = jax.random.randint(keys[0], (), 0, N_STN, dtype=jnp.int32)
        order = jax.random.permutation(keys[1], tickets).astype(jnp.int32)
        scores = jnp.where(owners == forced, within - CAP, order)
        ranked = jnp.argsort(scores, stable=True)[:2 * PB]
        local = jax.vmap(lambda k: jax.random.permutation(k, BO))(jax.random.split(keys[2], N_STN)).astype(jnp.int32)
        chosen_owner = owners[ranked]
        chosen_within = within[ranked]
        numbers = chosen_owner * BO + local[chosen_owner, chosen_within]
        numbers = jax.random.permutation(keys[3], numbers)
        return numbers.reshape(PB, 2)
    result = jax.vmap(one_reader)(jax.random.split(key, N_STN))
    return result.reshape(N_STN * PB, 2).astype(jnp.int32)


def place_ends(values, key, smallest, high):
    dims = values.shape
    index_at = [jax.random.randint(jax.random.fold_in(key, axis), (), 0, dims[axis]) for axis in range(len(dims))]
    values = values.at[tuple(index_at)].set(smallest)
    longest = dims.index(max(dims))
    index_at[longest] = (index_at[longest] + 1) % dims[longest]
    return values.at[tuple(index_at)].set(high)


def levels(key, extent, pieces, least, top_value):
    level = 1.0
    for dim, parts in pieces:
        draws = jax.random.uniform(jax.random.fold_in(jax.random.fold_in(key, 6), dim), (parts,), jnp.float32, least / len(pieces), top_value / len(pieces))
        level = level * jnp.repeat(jnp.exp(draws), extent[dim] // parts).reshape((-1,) + (1,) * (len(extent) - 1 - dim))
    return level


def scatter_about(own_key, shape, width, most, shards=(), held_as=jnp.bfloat16):
    entries = width * jax.random.normal(own_key, shape, jnp.float32)
    if shards:
        entries = entries * levels(own_key, shape, shards, -0.22, 0.18)
    return jnp.clip(entries, -most, most).astype(held_as)


def setup_inputs(seed: int = 0, part: int = 0) -> dict:
    key_of = jax.random.split(jax.random.key(seed), 4)
    own_keys = jax.random.split(jax.random.fold_in(key_of[3], part), 4)
    return {
        "spectra": scatter_about(own_keys[0], (HOURS, STATIONS, 2, F), 1.0, 6.0, ((0, 2), (1, 4), (3, 2))),
        "uptime": place_ends((jax.random.randint(own_keys[1], (HOURS, STATIONS), 0, 4) < 3).astype(jnp.int32), jax.random.fold_in(own_keys[1], 1), 0, 1),
        "pair_blocks": draw_pair_blocks(jax.random.fold_in(jax.random.fold_in(key_of[3], part), 71), part),
    }


def band_table(first, count, hour_total):
    half = L // 2
    freqs = first + jnp.arange(count, dtype=jnp.int32)
    lag_index = jnp.arange(L, dtype=jnp.int32)
    phase = freqs[:, None] * lag_index[None, :] % L
    angle = phase.astype(jnp.float32) * (2.0 * math.pi / L)
    weight = jnp.sin(math.pi * (freqs.astype(jnp.float32) + 0.5) / half) ** 2 / math.sqrt(hour_total * half)
    return jnp.concatenate([jnp.cos(angle) * weight[:, None], -jnp.sin(angle) * weight[:, None]], axis=0)

def reference(spectra, uptime, pair_blocks):
    masked = jnp.where(uptime[:, :, None, None] > 0, spectra, jnp.zeros_like(spectra)).astype(jnp.float32)
    blocks = masked.reshape(HOURS, NB, SB, 2, L // 2)
    table = band_table(0, L // 2, HOURS)

    def one_block(pair):
        first = lax.dynamic_index_in_dim(blocks, pair[0], 1, keepdims=False)
        second = lax.dynamic_index_in_dim(blocks, pair[1], 1, keepdims=False)
        real = jnp.einsum('hsf,htf->stf', first[:, :, 0], second[:, :, 0]) + jnp.einsum('hsf,htf->stf', first[:, :, 1], second[:, :, 1])
        imag = jnp.einsum('hsf,htf->stf', first[:, :, 1], second[:, :, 0]) - jnp.einsum('hsf,htf->stf', first[:, :, 0], second[:, :, 1])
        cross = jnp.concatenate([real, imag], axis=2).reshape(SB * SB, L)
        return jnp.dot(cross, table, precision=lax.Precision.HIGHEST, preferred_element_type=jnp.float32)
    stacks = lax.map(one_block, pair_blocks)
    return stacks.reshape(PAIRS, L)
```

```python
import functools
import math

import jax
import jax.numpy as jnp
from jax import lax
from jax.experimental import pallas as pl
from jax.experimental.pallas import tpu as pltpu
from jax.sharding import PartitionSpec as P

L = 1024
SB = 8
CAP = 2
LANES = 128


def exchange(x, axes, size, distance):
    return lax.ppermute(x, axes, [(i, i ^ distance) for i in range(size)])


def slots_kernel(readers, pairs_ref, uptime_ref, spectra_ref, *out_refs):
    me = lax.axis_index("stn")
    hours, stations = uptime_ref.shape
    freq_loc = spectra_ref.shape[3]
    owned = stations // SB
    reader_blocks = pairs_ref.shape[1] // readers
    rows = SB * 2
    up = uptime_ref[...].astype(jnp.float32).astype(jnp.bfloat16)
    for distance in range(readers):
        reader = me ^ distance
        slots = [jnp.int32(0)] * CAP
        found = jnp.int32(0)
        for entry in range(2 * reader_blocks):
            block = pairs_ref[entry % 2, reader * reader_blocks + entry // 2]
            mine = (block >= me * owned) & (block < (me + 1) * owned)
            for slot in range(CAP):
                slots[slot] = jnp.where(mine & (found == slot), block - me * owned, slots[slot])
            found = found + mine.astype(jnp.int32)
        for slot in range(CAP):
            base = slots[slot] * SB
            station = lax.broadcasted_iota(jnp.int32, (rows, stations), 1)
            row = lax.broadcasted_iota(jnp.int32, (rows, stations), 0)
            pick = (station == base + row // 2).astype(jnp.float32).astype(jnp.bfloat16)
            recorded = lax.dot_general(
                pick, up, (((1,), (1,)), ((), ())), preferred_element_type=jnp.float32
            )
            for hour in range(hours):
                values = spectra_ref[hour, pl.ds(base, SB)].astype(jnp.float32)
                values = values.reshape(rows, freq_loc)
                keep = jnp.broadcast_to(recorded[:, hour : hour + 1], (rows, freq_loc)) > 0
                out_refs[distance][slot, hour] = jnp.where(keep, values, 0.0).astype(jnp.bfloat16)


def cross_kernel(readers, parts, freq_parts, owned, pairs_ref, *refs):
    slot_refs, out_refs, blocks = refs[:readers], refs[readers : readers + parts], refs[-1]
    me = lax.axis_index("stn")
    mine = lax.axis_index("hour") * freq_parts + lax.axis_index("freq")
    reader_blocks = pairs_ref.shape[1] // readers
    _, chunks, hours, _, _ = blocks.shape
    wanted = [
        pairs_ref[entry % 2, me * reader_blocks + entry // 2] for entry in range(2 * reader_blocks)
    ]
    owners = [block // owned for block in wanted]
    for entry in range(2 * reader_blocks):
        slot = jnp.int32(0)
        for before in range(entry):
            slot = slot + (owners[before] == owners[entry]).astype(jnp.int32)
        slot = jnp.minimum(slot, CAP - 1)
        for distance in range(readers):

            @pl.when(owners[entry] == me ^ distance)
            def _(entry=entry, slot=slot, distance=distance):
                values = slot_refs[distance][slot].astype(jnp.float32)
                for chunk in range(blocks.shape[1]):
                    blocks[entry, chunk] = values[:, :, chunk * LANES : (chunk + 1) * LANES]

    part_rows = out_refs[0].shape[1] // SB
    for distance in range(parts):
        first_row = (mine ^ distance) * part_rows
        pair = first_row // SB
        station = first_row % SB
        for chunk in range(chunks):
            lanes = pl.ds(chunk * LANES, LANES)
            second = 2 * pair + 1
            second_re = [blocks[second, chunk, h, pl.ds(0, SB, stride=2)] for h in range(hours)]
            second_im = [blocks[second, chunk, h, pl.ds(1, SB, stride=2)] for h in range(hours)]
            for s in range(part_rows):
                real = jnp.zeros((SB, LANES), jnp.float32)
                imag = jnp.zeros((SB, LANES), jnp.float32)
                for h in range(hours):
                    first_re = blocks[2 * pair, chunk, h, pl.ds(2 * (station + s), 1)]
                    first_im = blocks[2 * pair, chunk, h, pl.ds(2 * (station + s) + 1, 1)]
                    real = real + first_re * second_re[h] + first_im * second_im[h]
                    imag = imag + first_im * second_re[h] - first_re * second_im[h]
                out_refs[distance][0, pl.ds(s * SB, SB), lanes] = real
                out_refs[distance][1, pl.ds(s * SB, SB), lanes] = imag


def table_kernel(hour_total, high_ref, low_ref):
    halves, twice, _ = high_ref.shape
    freq_loc = twice // 2
    half = L // 2
    turns = L // LANES
    sub = lax.broadcasted_iota(jnp.int32, (8, LANES), 0)
    lane = lax.broadcasted_iota(jnp.int32, (8, LANES), 1)
    steps = []
    for j in range(turns):
        turn = ((sub * j) % turns).astype(jnp.float32) * (2.0 * math.pi / turns)
        steps.append((jnp.cos(turn), jnp.sin(turn)))

    def rows(index, carry):
        c = index // (freq_loc // 8)
        r = index % (freq_loc // 8)
        freq = index * 8 + sub
        angle = ((freq * lane) % L).astype(jnp.float32) * (2.0 * math.pi / L)
        weight = jnp.sin(math.pi * (freq.astype(jnp.float32) + 0.5) / half) ** 2 / math.sqrt(
            hour_total * half
        )
        cos0 = jnp.cos(angle) * weight
        sin0 = jnp.sin(angle) * weight
        for j in range(turns):
            cj, sj = steps[j]
            lanes = pl.ds(j * LANES, LANES)
            for where, value in ((0, cos0 * cj - sin0 * sj), (freq_loc, -(sin0 * cj + cos0 * sj))):
                at = pl.ds(pl.multiple_of(where + r * 8, 8), 8)
                high = value.astype(jnp.bfloat16)
                high_ref[c, at, lanes] = high
                low_ref[c, at, lanes] = (value - high.astype(jnp.float32)).astype(jnp.bfloat16)
        return carry

    lax.fori_loop(0, halves * freq_loc // 8, rows, 0)


def lags_kernel(parts, freq_parts, high_ref, low_ref, *refs):
    part_refs, out_ref = refs[:parts], refs[-1]
    own = lax.axis_index("freq")
    total = None
    for c in range(freq_parts):
        cross = part_refs[c][...]
        for x in range(1, parts // freq_parts):
            cross = cross + part_refs[x * freq_parts + c][...]
        cross = jnp.concatenate([cross[0], cross[1]], axis=1)
        count = cross.shape[0]
        high = cross.astype(jnp.bfloat16)
        low = (cross - high.astype(jnp.float32)).astype(jnp.bfloat16)
        both = jnp.concatenate([high, low], axis=0)
        table = own ^ c
        by_high = jnp.dot(both, high_ref[table], preferred_element_type=jnp.float32)
        by_low = jnp.dot(high, low_ref[table], preferred_element_type=jnp.float32)
        term = by_high[:count] + (by_high[count:] + by_low)
        total = term if total is None else total + term
    out_ref[...] = total


def per_device(sizes, spectra, uptime, pair_blocks):
    readers, hour_parts, freq_parts = sizes
    hours, stations, _, freq_loc = spectra.shape
    parts = hour_parts * freq_parts
    reader_blocks = pair_blocks.shape[0] // readers
    part_pairs = reader_blocks * SB * SB // parts
    pairs = pair_blocks.T
    vmem = pl.BlockSpec(memory_space=pltpu.VMEM)
    smem = pl.BlockSpec(memory_space=pltpu.SMEM)
    limit = pltpu.CompilerParams(vmem_limit_bytes=32 * 1024 * 1024)

    slots = pl.pallas_call(
        functools.partial(slots_kernel, readers),
        out_shape=[jax.ShapeDtypeStruct((CAP, hours, 2 * SB, freq_loc), jnp.bfloat16)] * readers,
        in_specs=[smem, vmem, vmem],
        out_specs=[vmem] * readers,
        compiler_params=limit,
        name="slots",
    )(pairs, uptime, spectra)

    order = sorted(range(1, readers), key=lambda d: (d < readers // 2, d))
    arrived = [slots[0]] + [None] * (readers - 1)
    for distance in order:
        arrived[distance] = exchange(slots[distance], "stn", readers, distance)

    high, low = pl.pallas_call(
        functools.partial(table_kernel, hours * hour_parts),
        out_shape=[jax.ShapeDtypeStruct((freq_parts, 2 * freq_loc, L), jnp.bfloat16)] * 2,
        out_specs=[vmem] * 2,
        compiler_params=limit,
        cost_estimate=pl.CostEstimate(flops=20_000_000, bytes_accessed=4_000_000, transcendentals=0),
        name="band_table",
    )()

    cross = pl.pallas_call(
        functools.partial(cross_kernel, readers, parts, freq_parts, stations // SB),
        out_shape=[jax.ShapeDtypeStruct((2, part_pairs, freq_loc), jnp.float32)] * parts,
        in_specs=[smem] + [vmem] * readers,
        out_specs=[vmem] * parts,
        scratch_shapes=[pltpu.VMEM((2 * reader_blocks, freq_loc // LANES, hours, 2 * SB, LANES), jnp.float32)],
        compiler_params=limit,
        name="cross",
    )(pairs, *arrived)

    summed = [cross[0]] + [
        exchange(cross[distance], ("hour", "freq"), parts, distance) for distance in range(1, parts)
    ]

    return pl.pallas_call(
        functools.partial(lags_kernel, parts, freq_parts),
        out_shape=jax.ShapeDtypeStruct((part_pairs, L), jnp.float32),
        in_specs=[vmem] * (2 + parts),
        out_specs=vmem,
        compiler_params=limit,
        name="lags",
    )(high, low, *summed)


def solution(mesh):
    sizes = (mesh.shape["stn"], mesh.shape["hour"], mesh.shape["freq"])
    in_specs = (
        P(("groups", "hour"), "stn", None, "freq"),
        P(("groups", "hour"), "stn"),
        P("groups", None),
    )
    out_specs = P(("groups", "stn", "hour", "freq"), None)
    return jax.shard_map(
        functools.partial(per_device, sizes),
        mesh=mesh,
        in_specs=in_specs,
        out_specs=out_specs,
        check_vma=False,
    )
```

```python
import functools
import math

import jax
import jax.numpy as jnp
from jax import lax
from jax.experimental import pallas as pl
from jax.experimental.pallas import tpu as pltpu
from jax.sharding import PartitionSpec as P

L = 1024
SB = 8
CAP = 2
LANES = 128


def exchange(x, axes, size, distance):
    return lax.ppermute(x, axes, [(i, i ^ distance) for i in range(size)])


def slots_kernel(readers, pairs_hbm, uptime_hbm, spectra_hbm, *refs):
    out_refs, (pairs_out, pairs_ref, uptime_ref, spectra_ref, sems) = refs[:readers], refs[readers:]
    me = lax.axis_index("stn")
    hours, stations = uptime_ref.shape
    freq_loc = spectra_ref.shape[3]
    owned = stations // SB
    reader_blocks = pairs_ref.shape[1] // readers
    rows = SB * 2
    copies = [
        pltpu.make_async_copy(pairs_hbm, pairs_ref, sems.at[0]),
        pltpu.make_async_copy(uptime_hbm, uptime_ref, sems.at[1]),
        pltpu.make_async_copy(pairs_hbm, pairs_out, sems.at[2]),
    ] + [
        pltpu.make_async_copy(spectra_hbm.at[h], spectra_ref.at[h], sems.at[3 + h])
        for h in range(hours)
    ]
    for copy in copies:
        copy.start()
    for copy in copies:
        copy.wait()
    up = uptime_ref[...].astype(jnp.float32).astype(jnp.bfloat16)
    for distance in range(readers):
        reader = me ^ distance
        slots = [jnp.int32(0)] * CAP
        found = jnp.int32(0)
        for entry in range(2 * reader_blocks):
            block = pairs_ref[entry % 2, reader * reader_blocks + entry // 2]
            mine = (block >= me * owned) & (block < (me + 1) * owned)
            for slot in range(CAP):
                slots[slot] = jnp.where(mine & (found == slot), block - me * owned, slots[slot])
            found = found + mine.astype(jnp.int32)
        for slot in range(CAP):
            base = slots[slot] * SB
            station = lax.broadcasted_iota(jnp.int32, (rows, stations), 1)
            row = lax.broadcasted_iota(jnp.int32, (rows, stations), 0)
            pick = (station == base + row // 2).astype(jnp.float32).astype(jnp.bfloat16)
            recorded = lax.dot_general(
                pick, up, (((1,), (1,)), ((), ())), preferred_element_type=jnp.float32
            )
            for hour in range(hours):
                values = spectra_ref[hour, pl.ds(base, SB)].astype(jnp.float32)
                values = values.reshape(rows, freq_loc)
                keep = jnp.broadcast_to(recorded[:, hour : hour + 1], (rows, freq_loc)) > 0
                out_refs[distance][slot, hour] = jnp.where(keep, values, 0.0).astype(jnp.bfloat16)


def cross_kernel(order, parts, freq_parts, owned, pairs_ref, table_ref, *refs):
    del table_ref
    readers = len(order)
    slot_refs, out_refs, blocks = refs[:readers], refs[readers : readers + parts], refs[-1]
    me = lax.axis_index("stn")
    mine = lax.axis_index("hour") * freq_parts + lax.axis_index("freq")
    reader_blocks = pairs_ref.shape[1] // readers
    _, chunks, hours, _, _ = blocks.shape
    pairs = pairs_ref[...]
    side = lax.broadcasted_iota(jnp.int32, pairs.shape, 0)
    column = lax.broadcasted_iota(jnp.int32, pairs.shape, 1)
    wanted = []
    for entry in range(2 * reader_blocks):
        here = (side == entry % 2) & (column == me * reader_blocks + entry // 2)
        wanted.append(jnp.max(jnp.where(here, pairs, 0)))
    owners = [block // owned for block in wanted]
    for entry in range(2 * reader_blocks):
        slot = jnp.int32(0)
        for before in range(entry):
            slot = slot + (owners[before] == owners[entry]).astype(jnp.int32)
        slot = jnp.minimum(slot, CAP - 1)
        for slot_ref, distance in zip(slot_refs, order, strict=True):

            @pl.when(owners[entry] == me ^ distance)
            def _(entry=entry, slot=slot, slot_ref=slot_ref):
                values = slot_ref[slot].astype(jnp.float32)
                for chunk in range(blocks.shape[1]):
                    blocks[entry, chunk] = values[:, :, chunk * LANES : (chunk + 1) * LANES]

    part_rows = out_refs[0].shape[1] // SB
    for distance in range(parts):
        first_row = (mine ^ distance) * part_rows
        pair = first_row // SB
        station = first_row % SB
        for chunk in range(chunks):
            lanes = pl.ds(chunk * LANES, LANES)
            second = 2 * pair + 1
            second_re = [blocks[second, chunk, h, pl.ds(0, SB, stride=2)] for h in range(hours)]
            second_im = [blocks[second, chunk, h, pl.ds(1, SB, stride=2)] for h in range(hours)]
            for s in range(part_rows):
                real = jnp.zeros((SB, LANES), jnp.float32)
                imag = jnp.zeros((SB, LANES), jnp.float32)
                for h in range(hours):
                    first_re = blocks[2 * pair, chunk, h, pl.ds(2 * (station + s), 1)]
                    first_im = blocks[2 * pair, chunk, h, pl.ds(2 * (station + s) + 1, 1)]
                    real = real + first_re * second_re[h] + first_im * second_im[h]
                    imag = imag + first_im * second_re[h] - first_re * second_im[h]
                out_refs[distance][0, pl.ds(s * SB, SB), lanes] = real
                out_refs[distance][1, pl.ds(s * SB, SB), lanes] = imag


def table_kernel(hour_total, high_ref, low_ref):
    halves, twice, _ = high_ref.shape
    freq_loc = twice // 2
    half = L // 2
    turns = L // LANES
    sub = lax.broadcasted_iota(jnp.int32, (8, LANES), 0)
    lane = lax.broadcasted_iota(jnp.int32, (8, LANES), 1)
    steps = []
    for j in range(turns):
        turn = ((sub * j) % turns).astype(jnp.float32) * (2.0 * math.pi / turns)
        steps.append((jnp.cos(turn), jnp.sin(turn)))

    def rows(index, carry):
        c = index // (freq_loc // 8)
        r = index % (freq_loc // 8)
        freq = index * 8 + sub
        angle = ((freq * lane) % L).astype(jnp.float32) * (2.0 * math.pi / L)
        weight = jnp.sin(math.pi * (freq.astype(jnp.float32) + 0.5) / half) ** 2 / math.sqrt(
            hour_total * half
        )
        cos0 = jnp.cos(angle) * weight
        sin0 = jnp.sin(angle) * weight
        for j in range(turns):
            cj, sj = steps[j]
            lanes = pl.ds(j * LANES, LANES)
            for where, value in ((0, cos0 * cj - sin0 * sj), (freq_loc, -(sin0 * cj + cos0 * sj))):
                at = pl.ds(pl.multiple_of(where + r * 8, 8), 8)
                high = value.astype(jnp.bfloat16)
                high_ref[c, at, lanes] = high
                low_ref[c, at, lanes] = (value - high.astype(jnp.float32)).astype(jnp.bfloat16)
        return carry

    lax.fori_loop(0, halves * freq_loc // 8, rows, 0)


def lags_kernel(parts, freq_parts, high_ref, low_ref, *refs):
    part_refs, out_ref = refs[:parts], refs[-1]
    own = lax.axis_index("freq")
    total = None
    for c in range(freq_parts):
        cross = part_refs[c][...]
        for x in range(1, parts // freq_parts):
            cross = cross + part_refs[x * freq_parts + c][...]
        cross = jnp.concatenate([cross[0], cross[1]], axis=1)
        count = cross.shape[0]
        high = cross.astype(jnp.bfloat16)
        low = (cross - high.astype(jnp.float32)).astype(jnp.bfloat16)
        both = jnp.concatenate([high, low], axis=0)
        table = own ^ c
        by_high = jnp.dot(both, high_ref[table], preferred_element_type=jnp.float32)
        by_low = jnp.dot(high, low_ref[table], preferred_element_type=jnp.float32)
        term = by_high[:count] + (by_high[count:] + by_low)
        total = term if total is None else total + term
    out_ref[...] = total


def per_device(sizes, spectra, uptime, pair_blocks):
    readers, hour_parts, freq_parts = sizes
    hours, stations, _, freq_loc = spectra.shape
    parts = hour_parts * freq_parts
    reader_blocks = pair_blocks.shape[0] // readers
    part_pairs = reader_blocks * SB * SB // parts
    pairs = pair_blocks.T
    vmem = pl.BlockSpec(memory_space=pltpu.VMEM)
    whole = pl.BlockSpec(memory_space=pl.ANY)
    hbm = pl.BlockSpec(memory_space=pltpu.HBM)
    limit = pltpu.CompilerParams(vmem_limit_bytes=32 * 1024 * 1024)

    *slots, wanted = pl.pallas_call(
        functools.partial(slots_kernel, readers),
        out_shape=[jax.ShapeDtypeStruct((CAP, hours, 2 * SB, freq_loc), jnp.bfloat16)] * readers
        + [jax.ShapeDtypeStruct(pairs.shape, jnp.int32)],
        in_specs=[hbm] * 3,
        out_specs=[vmem] * (readers + 1),
        scratch_shapes=[
            pltpu.SMEM(pairs.shape, jnp.int32),
            pltpu.VMEM(uptime.shape, jnp.int32),
            pltpu.VMEM(spectra.shape, jnp.bfloat16),
            pltpu.SemaphoreType.DMA((3 + hours,)),
        ],
        compiler_params=limit,
        name="slots",
    )(pairs, uptime, spectra)

    order = sorted(range(1, readers), key=lambda d: (d < readers // 2, d))
    arrived = [exchange(slots[distance], "stn", readers, distance) for distance in order]

    high, low = pl.pallas_call(
        functools.partial(table_kernel, hours * hour_parts),
        out_shape=[jax.ShapeDtypeStruct((freq_parts, 2 * freq_loc, L), jnp.bfloat16)] * 2,
        out_specs=[vmem] * 2,
        compiler_params=limit,
        cost_estimate=pl.CostEstimate(flops=20_000_000, bytes_accessed=4_000_000, transcendentals=0),
        name="band_table",
    )()

    cross = pl.pallas_call(
        functools.partial(cross_kernel, order + [0], parts, freq_parts, stations // SB),
        out_shape=[jax.ShapeDtypeStruct((2, part_pairs, freq_loc), jnp.float32)] * parts,
        in_specs=[vmem, whole] + [vmem] * readers,
        out_specs=[vmem] * parts,
        scratch_shapes=[pltpu.VMEM((2 * reader_blocks, freq_loc // LANES, hours, 2 * SB, LANES), jnp.float32)],
        compiler_params=limit,
        name="cross",
    )(wanted, high, *arrived, slots[0])

    summed = [cross[0]] + [
        exchange(cross[distance], ("hour", "freq"), parts, distance) for distance in range(1, parts)
    ]

    return pl.pallas_call(
        functools.partial(lags_kernel, parts, freq_parts),
        out_shape=jax.ShapeDtypeStruct((part_pairs, L), jnp.float32),
        in_specs=[vmem] * (2 + parts),
        out_specs=vmem,
        compiler_params=limit,
        name="lags",
    )(high, low, *summed)


def solution(mesh):
    sizes = (mesh.shape["stn"], mesh.shape["hour"], mesh.shape["freq"])
    in_specs = (
        P(("groups", "hour"), "stn", None, "freq"),
        P(("groups", "hour"), "stn"),
        P("groups", None),
    )
    out_specs = P(("groups", "stn", "hour", "freq"), None)
    return jax.shard_map(
        functools.partial(per_device, sizes),
        mesh=mesh,
        in_specs=in_specs,
        out_specs=out_specs,
        check_vma=False,
    )
```

```python
import functools
import math

import jax
import jax.numpy as jnp
from jax import lax
from jax.experimental import pallas as pl
from jax.experimental.pallas import tpu as pltpu
from jax.sharding import PartitionSpec as P

L = 1024
SB = 8
CAP = 2
LANES = 128
QUARTER = L // 4


def exchange(x, axes, size, distance):
    return lax.ppermute(x, axes, [(i, i ^ distance) for i in range(size)])


def wanted_slots(pairs_ref, reader, me, reader_blocks, owned):
    starts = [jnp.int32(0)] * CAP
    found = jnp.int32(0)
    for entry in range(2 * reader_blocks):
        block = pairs_ref[entry % 2, reader * reader_blocks + entry // 2]
        mine = (block >= me * owned) & (block < (me + 1) * owned)
        for slot in range(CAP):
            starts[slot] = jnp.where(mine & (found == slot), (block - me * owned) * SB, starts[slot])
        found = found + mine.astype(jnp.int32)
    return starts


def recorded_rows(start, up):
    rows = 2 * SB
    station = lax.broadcasted_iota(jnp.int32, (rows, up.shape[1]), 1)
    row = lax.broadcasted_iota(jnp.int32, (rows, up.shape[1]), 0)
    pick = (station == start + row // 2).astype(jnp.float32).astype(jnp.bfloat16)
    return lax.dot_general(
        pick, up, (((1,), (1,)), ((), ())), preferred_element_type=jnp.float32
    )


def masked_rows(spectra_ref, hour, start, recorded):
    values = spectra_ref[hour, pl.ds(start, SB)].astype(jnp.float32)
    values = values.reshape(2 * SB, spectra_ref.shape[3])
    keep = jnp.broadcast_to(recorded[:, hour : hour + 1], values.shape) > 0
    return jnp.where(keep, values, 0.0).astype(jnp.bfloat16)


def write_slots(pairs_ref, up, spectra_ref, readers, distances, hours_ready, out_refs):
    me = lax.axis_index("stn")
    stations = up.shape[1]
    reader_blocks = pairs_ref.shape[1] // readers
    wanted = []
    for out_ref, distance in zip(out_refs, distances, strict=True):
        starts = wanted_slots(pairs_ref, me ^ distance, me, reader_blocks, stations // SB)
        for slot, start in enumerate(starts):
            wanted.append((out_ref, slot, start, recorded_rows(start, up)))
    for hour in range(spectra_ref.shape[0]):
        if hours_ready is not None:
            hours_ready[hour].wait()
        for out_ref, slot, start, recorded in wanted:
            out_ref[slot, hour] = masked_rows(spectra_ref, hour, start, recorded)


def send_kernel(readers, distances, pairs_hbm, uptime_hbm, spectra_hbm, *refs):
    out_refs, (pairs_out, pairs_ref, uptime_ref, spectra_ref, sems) = refs[:-5], refs[-5:]
    arguments = [
        pltpu.make_async_copy(pairs_hbm, pairs_ref, sems.at[0]),
        pltpu.make_async_copy(uptime_hbm, uptime_ref, sems.at[1]),
        pltpu.make_async_copy(pairs_hbm, pairs_out, sems.at[2]),
    ]
    spectra = [
        pltpu.make_async_copy(spectra_hbm.at[h], spectra_ref.at[h], sems.at[3 + h])
        for h in range(spectra_ref.shape[0])
    ]
    for copy in arguments + spectra:
        copy.start()
    for copy in arguments:
        copy.wait()
    up = uptime_ref[...].astype(jnp.float32).astype(jnp.bfloat16)
    write_slots(pairs_ref, up, spectra_ref, readers, distances, spectra, out_refs)


def prepare_kernel(readers, hour_total, pairs_ref, uptime_ref, spectra_ref, *refs):
    high_ref, low_ref, own_ref = refs
    up = uptime_ref[...].astype(jnp.float32).astype(jnp.bfloat16)
    write_slots(pairs_ref, up, spectra_ref, readers, [0], None, [own_ref])

    _, chunks, _, lags = high_ref.shape
    half = L // 2
    tall = 16
    groups = half // tall
    sub = lax.broadcasted_iota(jnp.int32, (tall, LANES), 0)
    lane = lax.broadcasted_iota(jnp.int32, (tall, LANES), 1)
    base_cos, base_sin = circle(sub * lane, L)
    group_cos, group_sin = circle(
        lax.broadcasted_iota(jnp.int32, (groups, LANES), 0)
        * lax.broadcasted_iota(jnp.int32, (groups, LANES), 1),
        L // tall,
    )
    steps = [circle(sub * j, L // LANES) for j in range(1, lags // LANES)]
    weight_cos, weight_sin = circle(2 * sub + 1, 2 * L)
    scale = 1.0 / math.sqrt(hour_total * half)
    for group in range(groups):
        turn_cos, turn_sin = group_cos[group : group + 1], group_sin[group : group + 1]
        quarter_turns = math.pi * tall * group / half
        weight = weight_sin * math.cos(quarter_turns) + weight_cos * math.sin(quarter_turns)
        weight = weight * weight * scale
        cos0 = (base_cos * turn_cos - base_sin * turn_sin) * weight
        sin0 = (base_sin * turn_cos + base_cos * turn_sin) * weight
        row = group % (LANES // tall) * tall
        at = group // (LANES // tall)
        for j in range(lags // LANES):
            real, imag = cos0, -sin0
            if j > 0:
                cj, sj = steps[j - 1]
                real, imag = cos0 * cj - sin0 * sj, -(sin0 * cj + cos0 * sj)
            for first, value in ((row, real), (LANES + row, imag)):
                where = (at // chunks, at % chunks, pl.ds(first, tall), pl.ds(j * LANES, LANES))
                high = value.astype(jnp.bfloat16)
                high_ref[where] = high
                low_ref[where] = (value - high.astype(jnp.float32)).astype(jnp.bfloat16)


def circle(step, steps):
    quarter = steps // 4
    step = step % steps
    turn = (step + quarter // 2) // quarter
    x = (step - turn * quarter).astype(jnp.float32) * (2.0 * math.pi / steps)
    y = x * x
    sin = x * (1.0 + y * (-1 / 6 + y * (1 / 120 + y * (-1 / 5040 + y * (1 / 362880)))))
    cos = 1.0 + y * (-1 / 2 + y * (1 / 24 + y * (-1 / 720 + y * (1 / 40320 - y * (1 / 3628800)))))
    turn = turn % 4
    odd = turn % 2 == 1
    out_cos, out_sin = jnp.where(odd, sin, cos), jnp.where(odd, cos, sin)
    out_cos = jnp.where((turn == 1) | (turn == 2), -out_cos, out_cos)
    out_sin = jnp.where((turn == 2) | (turn == 3), -out_sin, out_sin)
    return out_cos, out_sin


def cross_kernel(distances, parts, freq_parts, owned, pairs_ref, *refs):
    readers = len(distances)
    slot_refs, out_refs, blocks = refs[:readers], refs[readers : readers + parts], refs[-1]
    me = lax.axis_index("stn")
    mine = lax.axis_index("hour") * freq_parts + lax.axis_index("freq")
    reader_blocks = pairs_ref.shape[1] // readers
    _, chunks, hours, _, _ = blocks.shape
    pairs = pairs_ref[...]
    side = lax.broadcasted_iota(jnp.int32, pairs.shape, 0)
    column = lax.broadcasted_iota(jnp.int32, pairs.shape, 1)
    wanted = []
    for entry in range(2 * reader_blocks):
        here = (side == entry % 2) & (column == me * reader_blocks + entry // 2)
        wanted.append(jnp.max(jnp.where(here, pairs, 0)))
    owners = [block // owned for block in wanted]
    for entry in range(2 * reader_blocks):
        slot = jnp.int32(0)
        for before in range(entry):
            slot = slot + (owners[before] == owners[entry]).astype(jnp.int32)
        slot = jnp.minimum(slot, CAP - 1)
        for slot_ref, distance in zip(slot_refs, distances, strict=True):

            @pl.when(owners[entry] == me ^ distance)
            def _(entry=entry, slot=slot, slot_ref=slot_ref):
                values = slot_ref[slot].astype(jnp.float32)
                for chunk in range(chunks):
                    blocks[entry, chunk] = values[:, :, chunk * LANES : (chunk + 1) * LANES]

    part_rows = out_refs[0].shape[1] // SB
    for distance in range(parts):
        first_row = (mine ^ distance) * part_rows
        pair = first_row // SB
        station = first_row % SB
        for chunk in range(chunks):
            lanes = pl.ds(chunk * LANES, LANES)
            second = 2 * pair + 1
            second_re = [blocks[second, chunk, h, pl.ds(0, SB, stride=2)] for h in range(hours)]
            second_im = [blocks[second, chunk, h, pl.ds(1, SB, stride=2)] for h in range(hours)]
            for s in range(part_rows):
                real = jnp.zeros((SB, LANES), jnp.float32)
                imag = jnp.zeros((SB, LANES), jnp.float32)
                for h in range(hours):
                    first_re = blocks[2 * pair, chunk, h, pl.ds(2 * (station + s), 1)]
                    first_im = blocks[2 * pair, chunk, h, pl.ds(2 * (station + s) + 1, 1)]
                    real = real + first_re * second_re[h] + first_im * second_im[h]
                    imag = imag + first_im * second_re[h] - first_re * second_im[h]
                out_refs[distance][0, pl.ds(s * SB, SB), lanes] = real
                out_refs[distance][1, pl.ds(s * SB, SB), lanes] = imag


def lags_kernel(parts, freq_parts, high_ref, low_ref, *refs):
    part_refs, out_ref = refs[:-1], refs[-1]
    own = lax.axis_index("freq")
    count = out_ref.shape[0]
    phase = lax.broadcasted_iota(jnp.int32, (count, LANES), 1) % 4
    total = None
    for c in range(freq_parts):
        for chunk in range(high_ref.shape[1]):
            lanes = pl.ds(chunk * LANES, LANES)
            cross = part_refs[c][:, :, lanes]
            for x in range(1, parts // freq_parts):
                cross = cross + part_refs[x * freq_parts + c][:, :, lanes]
            real, imag = cross[0], cross[1]
            turned = []
            for q in range(4):
                step = (phase * q) % 4
                re = jnp.where(step % 2 == 0, real, imag)
                im = jnp.where(step % 2 == 0, imag, real)
                re = jnp.where((step == 1) | (step == 2), -re, re)
                im = jnp.where((step == 2) | (step == 3), -im, im)
                turned.append(jnp.concatenate([re, im], axis=1))
            turned = jnp.concatenate(turned, axis=0)
            high = turned.astype(jnp.bfloat16)
            low = (turned - high.astype(jnp.float32)).astype(jnp.bfloat16)
            table_high = high_ref[own ^ c, chunk]
            term = (
                jnp.dot(high, table_high, preferred_element_type=jnp.float32)
                + jnp.dot(low, table_high, preferred_element_type=jnp.float32)
                + jnp.dot(high, low_ref[own ^ c, chunk], preferred_element_type=jnp.float32)
            )
            total = term if total is None else total + term
    for q in range(4):
        out_ref[:, q * QUARTER : (q + 1) * QUARTER] = total[q * count : (q + 1) * count]


def per_device(sizes, spectra, uptime, pair_blocks):
    readers, hour_parts, freq_parts = sizes
    hours, stations, _, freq_loc = spectra.shape
    parts = hour_parts * freq_parts
    chunks = freq_loc // LANES
    reader_blocks = pair_blocks.shape[0] // readers
    part_pairs = reader_blocks * SB * SB // parts
    pairs = pair_blocks.T
    vmem = pl.BlockSpec(memory_space=pltpu.VMEM)
    smem = pl.BlockSpec(memory_space=pltpu.SMEM)
    hbm = pl.BlockSpec(memory_space=pltpu.HBM)
    limit = pltpu.CompilerParams(vmem_limit_bytes=32 * 1024 * 1024)
    slots_shape = jax.ShapeDtypeStruct((CAP, hours, 2 * SB, freq_loc), jnp.bfloat16)
    pairs_shape = jax.ShapeDtypeStruct(pairs.shape, jnp.int32)

    distances = [*range(readers // 2, readers), *range(1, readers // 2)]
    *sent, wanted = pl.pallas_call(
        functools.partial(send_kernel, readers, distances),
        out_shape=[slots_shape] * len(distances) + [pairs_shape],
        in_specs=[hbm] * 3,
        out_specs=[vmem] * (len(distances) + 1),
        scratch_shapes=[
            pltpu.SMEM(pairs.shape, jnp.int32),
            pltpu.VMEM(uptime.shape, jnp.int32),
            pltpu.VMEM(spectra.shape, jnp.bfloat16),
            pltpu.SemaphoreType.DMA((3 + hours,)),
        ],
        compiler_params=limit,
        name="send_slots",
    )(*[pltpu.with_memory_space_constraint(x, pltpu.HBM) for x in (pairs, uptime, spectra)])
    arrived = [exchange(slots, "stn", readers, d) for slots, d in zip(sent, distances)]

    table_shape = jax.ShapeDtypeStruct((freq_parts, chunks, 2 * LANES, QUARTER), jnp.bfloat16)
    high, low, own = pl.pallas_call(
        functools.partial(prepare_kernel, readers, hours * hour_parts),
        out_shape=[table_shape] * 2 + [slots_shape],
        in_specs=[smem, vmem, vmem],
        out_specs=[vmem] * 3,
        compiler_params=limit,
        cost_estimate=pl.CostEstimate(flops=5_000_000, bytes_accessed=2_000_000, transcendentals=0),
        name="own_slots_and_table",
    )(wanted, uptime, spectra)

    cross = pl.pallas_call(
        functools.partial(cross_kernel, [*distances, 0], parts, freq_parts, stations // SB),
        out_shape=[jax.ShapeDtypeStruct((2, part_pairs, freq_loc), jnp.float32)] * parts,
        in_specs=[vmem] * (1 + readers),
        out_specs=[vmem] * parts,
        scratch_shapes=[
            pltpu.VMEM((2 * reader_blocks, chunks, hours, 2 * SB, LANES), jnp.float32)
        ],
        compiler_params=limit,
        name="cross",
    )(wanted, *arrived, own)
    summed = [cross[0]] + [
        exchange(cross[distance], ("hour", "freq"), parts, distance) for distance in range(1, parts)
    ]

    return pl.pallas_call(
        functools.partial(lags_kernel, parts, freq_parts),
        out_shape=jax.ShapeDtypeStruct((part_pairs, L), jnp.float32),
        in_specs=[vmem] * (2 + parts),
        out_specs=vmem,
        compiler_params=limit,
        name="lags",
    )(high, low, *summed)


def solution(mesh):
    sizes = (mesh.shape["stn"], mesh.shape["hour"], mesh.shape["freq"])
    in_specs = (
        P(("groups", "hour"), "stn", None, "freq"),
        P(("groups", "hour"), "stn"),
        P("groups", None),
    )
    out_specs = P(("groups", "stn", "hour", "freq"), None)
    return jax.shard_map(
        functools.partial(per_device, sizes),
        mesh=mesh,
        in_specs=in_specs,
        out_specs=out_specs,
        check_vma=False,
    )
```

```python
import functools
import math

import jax
import jax.numpy as jnp
from jax import lax
from jax.experimental import pallas as pl
from jax.experimental.pallas import tpu as pltpu
from jax.sharding import PartitionSpec as P

L = 1024
SB = 8
CAP = 2
LANES = 128
QUARTER = L // 4


def shift(x, axis, size, distance):
    return lax.ppermute(x, axis, [(i, (i + distance) % size) for i in range(size)])


def exchange(x, axes, size, distance):
    return lax.ppermute(x, axes, [(i, i ^ distance) for i in range(size)])


def wanted_slots(pairs_ref, reader, me, reader_blocks, owned):
    starts = [jnp.int32(0)] * CAP
    found = jnp.int32(0)
    for entry in range(2 * reader_blocks):
        block = pairs_ref[entry % 2, reader * reader_blocks + entry // 2]
        mine = (block >= me * owned) & (block < (me + 1) * owned)
        for slot in range(CAP):
            starts[slot] = jnp.where(mine & (found == slot), (block - me * owned) * SB, starts[slot])
        found = found + mine.astype(jnp.int32)
    return starts


def recorded_rows(start, up):
    rows = 2 * SB
    station = lax.broadcasted_iota(jnp.int32, (rows, up.shape[1]), 1)
    row = lax.broadcasted_iota(jnp.int32, (rows, up.shape[1]), 0)
    pick = (station == start + row // 2).astype(jnp.float32).astype(jnp.bfloat16)
    return lax.dot_general(
        pick, up, (((1,), (1,)), ((), ())), preferred_element_type=jnp.float32
    )


def masked_rows(spectra_ref, hour, start, recorded):
    values = spectra_ref[hour, pl.ds(start, SB)].astype(jnp.float32)
    values = values.reshape(2 * SB, spectra_ref.shape[3])
    keep = jnp.broadcast_to(recorded[:, hour : hour + 1], values.shape) > 0
    return jnp.where(keep, values, 0.0).astype(jnp.bfloat16)


def send_kernel(readers, distances, pairs_hbm, uptime_hbm, spectra_hbm, *refs):
    slot_refs, (pairs_ref, uptime_ref, spectra_ref, sems) = refs[:-4], refs[-4:]
    me = lax.axis_index("stn")
    hours, stations = uptime_ref.shape
    reader_blocks = pairs_ref.shape[1] // readers
    arguments = [
        pltpu.make_async_copy(pairs_hbm, pairs_ref, sems.at[0]),
        pltpu.make_async_copy(uptime_hbm, uptime_ref, sems.at[1]),
    ]
    pieces = 2 if hours % 2 == 0 else 1
    count = hours // pieces
    spectra = []
    for piece in range(pieces):
        some = pl.ds(piece * count, count)
        spectra.append(
            pltpu.make_async_copy(spectra_hbm.at[some], spectra_ref.at[some], sems.at[2 + piece])
        )
    for copy in arguments + spectra:
        copy.start()
    for copy in arguments:
        copy.wait()
    up = uptime_ref[...].astype(jnp.float32).astype(jnp.bfloat16)
    wanted = []
    for slot_ref, distance in zip(slot_refs, distances, strict=True):
        reader = (me + distance) % readers
        starts = wanted_slots(pairs_ref, reader, me, reader_blocks, stations // SB)
        for slot, start in enumerate(starts):
            wanted.append((slot_ref, slot, start, recorded_rows(start, up)))
    for hour in range(hours):
        if hour % count == 0:
            spectra[hour // count].wait()
        for slot_ref, slot, start, recorded in wanted:
            slot_ref[slot, hour] = masked_rows(spectra_ref, hour, start, recorded)


def table_kernel(hour_total, wanted_ref, high_ref, low_ref):
    del wanted_ref
    _, rows, lags = high_ref.shape
    half = L // 2
    tall = 16
    groups = half // tall
    sub = lax.broadcasted_iota(jnp.int32, (tall, LANES), 0)
    lane = lax.broadcasted_iota(jnp.int32, (tall, LANES), 1)
    base_cos, base_sin = circle(sub * lane, L)
    group_cos, group_sin = circle(
        lax.broadcasted_iota(jnp.int32, (groups, LANES), 0)
        * lax.broadcasted_iota(jnp.int32, (groups, LANES), 1),
        L // tall,
    )
    steps = [circle(sub * j, L // LANES) for j in range(1, lags // LANES)]
    weight_cos, weight_sin = circle(2 * sub + 1, 2 * L)
    scale = 1.0 / math.sqrt(hour_total * half)
    for group in range(groups):
        turn_cos, turn_sin = group_cos[group : group + 1], group_sin[group : group + 1]
        quarter_turns = math.pi * tall * group / half
        weight = weight_sin * math.cos(quarter_turns) + weight_cos * math.sin(quarter_turns)
        weight = weight * weight * scale
        cos0 = (base_cos * turn_cos - base_sin * turn_sin) * weight
        sin0 = (base_sin * turn_cos + base_cos * turn_sin) * weight
        chunk, row = divmod(group * tall, LANES)
        at, chunk = divmod(chunk * 2 * LANES, rows)
        for j in range(lags // LANES):
            real, imag = cos0, -sin0
            if j > 0:
                cj, sj = steps[j - 1]
                real, imag = cos0 * cj - sin0 * sj, -(sin0 * cj + cos0 * sj)
            for first, value in ((chunk + row, real), (chunk + LANES + row, imag)):
                where = (at, pl.ds(first, tall), pl.ds(j * LANES, LANES))
                high = value.astype(jnp.bfloat16)
                high_ref[where] = high
                low_ref[where] = (value - high.astype(jnp.float32)).astype(jnp.bfloat16)


def circle(step, steps):
    quarter = steps // 4
    step = step % steps
    turn = (step + quarter // 2) // quarter
    x = (step - turn * quarter).astype(jnp.float32) * (2.0 * math.pi / steps)
    y = x * x
    sin = x * (1.0 + y * (-1 / 6 + y * (1 / 120 + y * (-1 / 5040 + y * (1 / 362880)))))
    cos = 1.0 + y * (-1 / 2 + y * (1 / 24 + y * (-1 / 720 + y * (1 / 40320 - y * (1 / 3628800)))))
    turn = turn % 4
    odd = turn % 2 == 1
    out_cos, out_sin = jnp.where(odd, sin, cos), jnp.where(odd, cos, sin)
    out_cos = jnp.where((turn == 1) | (turn == 2), -out_cos, out_cos)
    out_sin = jnp.where((turn == 2) | (turn == 3), -out_sin, out_sin)
    return out_cos, out_sin


def cross_kernel(distances, parts, freq_parts, owned, pairs_ref, *refs):
    readers = len(distances)
    slot_refs, out_refs, blocks = refs[:readers], refs[readers : readers + parts], refs[-1]
    me = lax.axis_index("stn")
    mine = lax.axis_index("hour") * freq_parts + lax.axis_index("freq")
    reader_blocks = pairs_ref.shape[1] // readers
    _, chunks, hours, _, _ = blocks.shape
    wanted = []
    for entry in range(2 * reader_blocks):
        wanted.append(pairs_ref[entry % 2, me * reader_blocks + entry // 2])
    owners = [block // owned for block in wanted]
    for entry in range(2 * reader_blocks):
        slot = jnp.int32(0)
        for before in range(entry):
            slot = slot + (owners[before] == owners[entry]).astype(jnp.int32)
        slot = jnp.minimum(slot, CAP - 1)
        for slot_ref, distance in zip(slot_refs, distances, strict=True):

            @pl.when(owners[entry] == (me + readers - distance) % readers)
            def _(entry=entry, slot=slot, slot_ref=slot_ref):
                values = slot_ref[slot].astype(jnp.float32)
                for chunk in range(chunks):
                    blocks[entry, chunk] = values[:, :, chunk * LANES : (chunk + 1) * LANES]

    part_rows = out_refs[0].shape[1] // SB
    for distance in range(parts):
        first_row = (mine ^ distance) * part_rows
        pair = first_row // SB
        station = first_row % SB
        for chunk in range(chunks):
            lanes = pl.ds(chunk * LANES, LANES)
            second = 2 * pair + 1
            second_re = [blocks[second, chunk, h, pl.ds(0, SB, stride=2)] for h in range(hours)]
            second_im = [blocks[second, chunk, h, pl.ds(1, SB, stride=2)] for h in range(hours)]
            for s in range(part_rows):
                real = jnp.zeros((SB, LANES), jnp.float32)
                imag = jnp.zeros((SB, LANES), jnp.float32)
                for h in range(hours):
                    first_re = blocks[2 * pair, chunk, h, pl.ds(2 * (station + s), 1)]
                    first_im = blocks[2 * pair, chunk, h, pl.ds(2 * (station + s) + 1, 1)]
                    real = real + first_re * second_re[h] + first_im * second_im[h]
                    imag = imag + first_im * second_re[h] - first_re * second_im[h]
                out_refs[distance][0, pl.ds(s * SB, SB), lanes] = real
                out_refs[distance][1, pl.ds(s * SB, SB), lanes] = imag


def lags_kernel(parts, freq_parts, high_ref, low_ref, *refs):
    part_refs, out_ref = refs[:-1], refs[-1]
    own = lax.axis_index("freq")
    count = out_ref.shape[0]
    chunks = part_refs[0].shape[2] // LANES
    phase = lax.broadcasted_iota(jnp.int32, (count, LANES), 1) % 4
    total = None
    for c in range(freq_parts):
        highs, lows = [], []
        for chunk in range(chunks):
            lanes = pl.ds(chunk * LANES, LANES)
            cross = part_refs[c][:, :, lanes]
            for x in range(1, parts // freq_parts):
                cross = cross + part_refs[x * freq_parts + c][:, :, lanes]
            real, imag = cross[0], cross[1]
            turned = []
            for q in range(4):
                step = (phase * q) % 4
                re = jnp.where(step % 2 == 0, real, imag)
                im = jnp.where(step % 2 == 0, imag, real)
                re = jnp.where((step == 1) | (step == 2), -re, re)
                im = jnp.where((step == 2) | (step == 3), -im, im)
                turned.append(jnp.concatenate([re, im], axis=1))
            turned = jnp.concatenate(turned, axis=0)
            high = turned.astype(jnp.bfloat16)
            highs.append(high)
            lows.append((turned - high.astype(jnp.float32)).astype(jnp.bfloat16))
        high, low = jnp.concatenate(highs, axis=1), jnp.concatenate(lows, axis=1)
        both = jnp.concatenate([high, low], axis=0)
        by_high = jnp.dot(both, high_ref[own ^ c], preferred_element_type=jnp.float32)
        by_low = jnp.dot(high, low_ref[own ^ c], preferred_element_type=jnp.float32)
        term = by_high[: 4 * count] + (by_high[4 * count :] + by_low)
        total = term if total is None else total + term
    for q in range(4):
        out_ref[:, q * QUARTER : (q + 1) * QUARTER] = total[q * count : (q + 1) * count]


def per_device(sizes, spectra, uptime, pair_blocks):
    readers, hour_parts, freq_parts = sizes
    hours, stations, _, freq_loc = spectra.shape
    parts = hour_parts * freq_parts
    chunks = freq_loc // LANES
    reader_blocks = pair_blocks.shape[0] // readers
    part_pairs = reader_blocks * SB * SB // parts
    pairs = pair_blocks.T
    vmem = pl.BlockSpec(memory_space=pltpu.VMEM)
    smem = pl.BlockSpec(memory_space=pltpu.SMEM)
    hbm = pl.BlockSpec(memory_space=pltpu.HBM)
    limit = pltpu.CompilerParams(vmem_limit_bytes=32 * 1024 * 1024)
    slots_shape = jax.ShapeDtypeStruct((CAP, hours, 2 * SB, freq_loc), jnp.bfloat16)

    distances = sorted(range(1, readers), key=lambda d: (abs(2 * d - readers), -d))
    *sent, own, wanted = pl.pallas_call(
        functools.partial(send_kernel, readers, [*distances, 0]),
        out_shape=[slots_shape] * (len(distances) + 1) + [pltpu.SMEM(pairs.shape, jnp.int32)],
        in_specs=[hbm] * 3,
        out_specs=[vmem] * (len(distances) + 1) + [smem],
        scratch_shapes=[
            pltpu.VMEM(uptime.shape, jnp.int32),
            pltpu.VMEM(spectra.shape, jnp.bfloat16),
            pltpu.SemaphoreType.DMA((4,)),
        ],
        compiler_params=limit,
        name="send_slots",
    )(*[pltpu.with_memory_space_constraint(x, pltpu.HBM) for x in (pairs, uptime, spectra)])
    arrived = [shift(slots, "stn", readers, d) for slots, d in zip(sent, distances)]

    table_shape = jax.ShapeDtypeStruct((freq_parts, 2 * freq_loc, QUARTER), jnp.bfloat16)
    high, low = pl.pallas_call(
        functools.partial(table_kernel, hours * hour_parts),
        out_shape=[table_shape] * 2,
        in_specs=[smem],
        out_specs=[vmem] * 2,
        compiler_params=limit,
        cost_estimate=pl.CostEstimate(flops=5_000_000, bytes_accessed=2_000_000, transcendentals=0),
        name="band_table",
    )(pltpu.with_memory_space_constraint(wanted, pltpu.SMEM))

    cross = pl.pallas_call(
        functools.partial(cross_kernel, [*distances, 0], parts, freq_parts, stations // SB),
        out_shape=[jax.ShapeDtypeStruct((2, part_pairs, freq_loc), jnp.float32)] * parts,
        in_specs=[smem] + [vmem] * readers,
        out_specs=[vmem] * parts,
        scratch_shapes=[
            pltpu.VMEM((2 * reader_blocks, chunks, hours, 2 * SB, LANES), jnp.float32)
        ],
        compiler_params=limit,
        name="cross",
    )(pltpu.with_memory_space_constraint(wanted, pltpu.SMEM), *arrived, own)
    summed = [cross[0]] + [
        exchange(cross[distance], ("hour", "freq"), parts, distance) for distance in range(1, parts)
    ]

    return pl.pallas_call(
        functools.partial(lags_kernel, parts, freq_parts),
        out_shape=jax.ShapeDtypeStruct((part_pairs, L), jnp.float32),
        in_specs=[vmem] * (2 + parts),
        out_specs=vmem,
        compiler_params=limit,
        name="lags",
    )(high, low, *summed)


def solution(mesh):
    sizes = (mesh.shape["stn"], mesh.shape["hour"], mesh.shape["freq"])
    in_specs = (
        P(("groups", "hour"), "stn", None, "freq"),
        P(("groups", "hour"), "stn"),
        P("groups", None),
    )
    out_specs = P(("groups", "stn", "hour", "freq"), None)
    return jax.shard_map(
        functools.partial(per_device, sizes),
        mesh=mesh,
        in_specs=in_specs,
        out_specs=out_specs,
        check_vma=False,
    )
```

```python
import functools
import math

import jax
import jax.numpy as jnp
from jax import lax
from jax.experimental import pallas as pl
from jax.experimental.pallas import tpu as pltpu
from jax.sharding import PartitionSpec as P

L = 1024
SB = 8
CAP = 2
LANES = 128
QUARTER = L // 4


def station_rounds(readers):
    ring = [i // 2 if i % 2 == 0 else readers - 1 - i // 2 for i in range(readers)]
    shifts = [*range(1, readers, 2), *range(2, readers, 2)]
    return [[ring[(ring.index(s) + d) % readers] for s in range(readers)] for d in shifts]


def pick(table, index):
    value = jnp.int32(table[0])
    for position, entry in enumerate(table):
        value = jnp.where(index == position, jnp.int32(entry), value)
    return value


def exchange(x, axes, size, distance):
    return lax.ppermute(x, axes, [(i, i ^ distance) for i in range(size)])


def wanted_slots(pairs_ref, reader, me, reader_blocks, owned):
    starts = [jnp.int32(0)] * CAP
    found = jnp.int32(0)
    for entry in range(2 * reader_blocks):
        block = pairs_ref[entry % 2, reader * reader_blocks + entry // 2]
        mine = (block >= me * owned) & (block < (me + 1) * owned)
        for slot in range(CAP):
            starts[slot] = jnp.where(mine & (found == slot), (block - me * owned) * SB, starts[slot])
        found = found + mine.astype(jnp.int32)
    return starts


def recorded_rows(start, up):
    rows = 2 * SB
    station = lax.broadcasted_iota(jnp.int32, (rows, up.shape[1]), 1)
    row = lax.broadcasted_iota(jnp.int32, (rows, up.shape[1]), 0)
    pick = (station == start + row // 2).astype(jnp.float32).astype(jnp.bfloat16)
    return lax.dot_general(
        pick, up, (((1,), (1,)), ((), ())), preferred_element_type=jnp.float32
    )


def masked_rows(spectra_ref, hour, start, recorded):
    values = spectra_ref[hour, pl.ds(start, SB)].astype(jnp.float32)
    values = values.reshape(2 * SB, spectra_ref.shape[3])
    keep = jnp.broadcast_to(recorded[:, hour : hour + 1], values.shape) > 0
    return jnp.where(keep, values, 0.0).astype(jnp.bfloat16)


def send_kernel(readers, rounds, pairs_hbm, uptime_hbm, spectra_hbm, *refs):
    slot_refs, (pairs_ref, uptime_ref, spectra_ref, sems) = refs[:-4], refs[-4:]
    me = lax.axis_index("stn")
    hours, stations = uptime_ref.shape
    reader_blocks = pairs_ref.shape[1] // readers
    arguments = [
        pltpu.make_async_copy(pairs_hbm, pairs_ref, sems.at[0]),
        pltpu.make_async_copy(uptime_hbm, uptime_ref, sems.at[1]),
    ]
    pieces = 2 if hours % 2 == 0 else 1
    count = hours // pieces
    spectra = []
    for piece in range(pieces):
        some = pl.ds(piece * count, count)
        spectra.append(
            pltpu.make_async_copy(spectra_hbm.at[some], spectra_ref.at[some], sems.at[2 + piece])
        )
    for copy in arguments + spectra:
        copy.start()
    for copy in arguments:
        copy.wait()
    up = uptime_ref[...].astype(jnp.float32).astype(jnp.bfloat16)
    wanted = []
    for slot_ref, targets in zip(slot_refs, rounds, strict=True):
        reader = pick(targets, me)
        starts = wanted_slots(pairs_ref, reader, me, reader_blocks, stations // SB)
        for slot, start in enumerate(starts):
            wanted.append((slot_ref, slot, start, recorded_rows(start, up)))
    for hour in range(hours):
        if hour % count == 0:
            spectra[hour // count].wait()
        for slot_ref, slot, start, recorded in wanted:
            slot_ref[slot, hour] = masked_rows(spectra_ref, hour, start, recorded)


def table_kernel(hour_total, wanted_ref, high_ref, low_ref):
    del wanted_ref
    _, rows, lags = high_ref.shape
    half = L // 2
    tall = 16
    groups = half // tall
    sub = lax.broadcasted_iota(jnp.int32, (tall, LANES), 0)
    lane = lax.broadcasted_iota(jnp.int32, (tall, LANES), 1)
    base_cos, base_sin = circle(sub * lane, L)
    group_cos, group_sin = circle(
        lax.broadcasted_iota(jnp.int32, (groups, LANES), 0)
        * lax.broadcasted_iota(jnp.int32, (groups, LANES), 1),
        L // tall,
    )
    steps = [circle(sub * j, L // LANES) for j in range(1, lags // LANES)]
    weight_cos, weight_sin = circle(2 * sub + 1, 2 * L)
    scale = 1.0 / math.sqrt(hour_total * half)
    for group in range(groups):
        turn_cos, turn_sin = group_cos[group : group + 1], group_sin[group : group + 1]
        quarter_turns = math.pi * tall * group / half
        weight = weight_sin * math.cos(quarter_turns) + weight_cos * math.sin(quarter_turns)
        weight = weight * weight * scale
        cos0 = (base_cos * turn_cos - base_sin * turn_sin) * weight
        sin0 = (base_sin * turn_cos + base_cos * turn_sin) * weight
        chunk, row = divmod(group * tall, LANES)
        at, chunk = divmod(chunk * 2 * LANES, rows)
        for j in range(lags // LANES):
            real, imag = cos0, -sin0
            if j > 0:
                cj, sj = steps[j - 1]
                real, imag = cos0 * cj - sin0 * sj, -(sin0 * cj + cos0 * sj)
            for first, value in ((chunk + row, real), (chunk + LANES + row, imag)):
                where = (at, pl.ds(first, tall), pl.ds(j * LANES, LANES))
                high = value.astype(jnp.bfloat16)
                high_ref[where] = high
                low_ref[where] = (value - high.astype(jnp.float32)).astype(jnp.bfloat16)


def circle(step, steps):
    quarter = steps // 4
    step = step % steps
    turn = (step + quarter // 2) // quarter
    x = (step - turn * quarter).astype(jnp.float32) * (2.0 * math.pi / steps)
    y = x * x
    sin = x * (1.0 + y * (-1 / 6 + y * (1 / 120 + y * (-1 / 5040 + y * (1 / 362880)))))
    cos = 1.0 + y * (-1 / 2 + y * (1 / 24 + y * (-1 / 720 + y * (1 / 40320 - y * (1 / 3628800)))))
    turn = turn % 4
    odd = turn % 2 == 1
    out_cos, out_sin = jnp.where(odd, sin, cos), jnp.where(odd, cos, sin)
    out_cos = jnp.where((turn == 1) | (turn == 2), -out_cos, out_cos)
    out_sin = jnp.where((turn == 2) | (turn == 3), -out_sin, out_sin)
    return out_cos, out_sin


def cross_kernel(rounds, parts, freq_parts, owned, pairs_ref, *refs):
    readers = len(rounds[0])
    count = len(rounds)
    slot_refs, out_refs, blocks = refs[:count], refs[count : count + parts], refs[-1]
    me = lax.axis_index("stn")
    mine = lax.axis_index("hour") * freq_parts + lax.axis_index("freq")
    reader_blocks = pairs_ref.shape[1] // readers
    _, chunks, hours, _, _ = blocks.shape
    wanted = []
    for entry in range(2 * reader_blocks):
        wanted.append(pairs_ref[entry % 2, me * reader_blocks + entry // 2])
    owners = [block // owned for block in wanted]
    for entry in range(2 * reader_blocks):
        slot = jnp.int32(0)
        for before in range(entry):
            slot = slot + (owners[before] == owners[entry]).astype(jnp.int32)
        slot = jnp.minimum(slot, CAP - 1)
        for slot_ref, sources in zip(slot_refs, rounds, strict=True):

            @pl.when(owners[entry] == pick(sources, me))
            def _(entry=entry, slot=slot, slot_ref=slot_ref):
                values = slot_ref[slot].astype(jnp.float32)
                for chunk in range(chunks):
                    blocks[entry, chunk] = values[:, :, chunk * LANES : (chunk + 1) * LANES]

    part_rows = out_refs[0].shape[1] // SB
    for distance in range(parts):
        first_row = (mine ^ distance) * part_rows
        pair = first_row // SB
        station = first_row % SB
        for chunk in range(chunks):
            lanes = pl.ds(chunk * LANES, LANES)
            second = 2 * pair + 1
            second_re = [blocks[second, chunk, h, pl.ds(0, SB, stride=2)] for h in range(hours)]
            second_im = [blocks[second, chunk, h, pl.ds(1, SB, stride=2)] for h in range(hours)]
            for s in range(part_rows):
                real = jnp.zeros((SB, LANES), jnp.float32)
                imag = jnp.zeros((SB, LANES), jnp.float32)
                for h in range(hours):
                    first_re = blocks[2 * pair, chunk, h, pl.ds(2 * (station + s), 1)]
                    first_im = blocks[2 * pair, chunk, h, pl.ds(2 * (station + s) + 1, 1)]
                    real = real + first_re * second_re[h] + first_im * second_im[h]
                    imag = imag + first_im * second_re[h] - first_re * second_im[h]
                out_refs[distance][0, pl.ds(s * SB, SB), lanes] = real
                out_refs[distance][1, pl.ds(s * SB, SB), lanes] = imag


def lags_kernel(parts, freq_parts, high_ref, low_ref, *refs):
    part_refs, out_ref = refs[:-1], refs[-1]
    own = lax.axis_index("freq")
    count = out_ref.shape[0]
    chunks = part_refs[0].shape[2] // LANES
    phase = lax.broadcasted_iota(jnp.int32, (count, LANES), 1) % 4
    total = None
    for c in range(freq_parts):
        highs, lows = [], []
        for chunk in range(chunks):
            lanes = pl.ds(chunk * LANES, LANES)
            cross = part_refs[c][:, :, lanes]
            for x in range(1, parts // freq_parts):
                cross = cross + part_refs[x * freq_parts + c][:, :, lanes]
            real, imag = cross[0], cross[1]
            turned = []
            for q in range(4):
                step = (phase * q) % 4
                re = jnp.where(step % 2 == 0, real, imag)
                im = jnp.where(step % 2 == 0, imag, real)
                re = jnp.where((step == 1) | (step == 2), -re, re)
                im = jnp.where((step == 2) | (step == 3), -im, im)
                turned.append(jnp.concatenate([re, im], axis=1))
            turned = jnp.concatenate(turned, axis=0)
            high = turned.astype(jnp.bfloat16)
            highs.append(high)
            lows.append((turned - high.astype(jnp.float32)).astype(jnp.bfloat16))
        high, low = jnp.concatenate(highs, axis=1), jnp.concatenate(lows, axis=1)
        both = jnp.concatenate([high, low], axis=0)
        by_high = jnp.dot(both, high_ref[own ^ c], preferred_element_type=jnp.float32)
        by_low = jnp.dot(high, low_ref[own ^ c], preferred_element_type=jnp.float32)
        term = by_high[: 4 * count] + (by_high[4 * count :] + by_low)
        total = term if total is None else total + term
    for q in range(4):
        out_ref[:, q * QUARTER : (q + 1) * QUARTER] = total[q * count : (q + 1) * count]


def per_device(sizes, spectra, uptime, pair_blocks):
    readers, hour_parts, freq_parts = sizes
    hours, stations, _, freq_loc = spectra.shape
    parts = hour_parts * freq_parts
    chunks = freq_loc // LANES
    reader_blocks = pair_blocks.shape[0] // readers
    part_pairs = reader_blocks * SB * SB // parts
    pairs = pair_blocks.T
    vmem = pl.BlockSpec(memory_space=pltpu.VMEM)
    smem = pl.BlockSpec(memory_space=pltpu.SMEM)
    hbm = pl.BlockSpec(memory_space=pltpu.HBM)
    limit = pltpu.CompilerParams(vmem_limit_bytes=32 * 1024 * 1024)
    slots_shape = jax.ShapeDtypeStruct((CAP, hours, 2 * SB, freq_loc), jnp.bfloat16)

    rounds = station_rounds(readers)
    here = [*range(readers)]
    *sent, own, wanted = pl.pallas_call(
        functools.partial(send_kernel, readers, [*rounds, here]),
        out_shape=[slots_shape] * (len(rounds) + 1) + [pltpu.SMEM(pairs.shape, jnp.int32)],
        in_specs=[hbm] * 3,
        out_specs=[vmem] * (len(rounds) + 1) + [smem],
        scratch_shapes=[
            pltpu.VMEM(uptime.shape, jnp.int32),
            pltpu.VMEM(spectra.shape, jnp.bfloat16),
            pltpu.SemaphoreType.DMA((4,)),
        ],
        compiler_params=limit,
        name="send_slots",
    )(*[pltpu.with_memory_space_constraint(x, pltpu.HBM) for x in (pairs, uptime, spectra)])
    arrived = [
        lax.ppermute(slots, "stn", [*enumerate(targets)])
        for slots, targets in zip(sent, rounds, strict=True)
    ]
    sources = [[targets.index(t) for t in range(readers)] for targets in rounds]

    table_shape = jax.ShapeDtypeStruct((freq_parts, 2 * freq_loc, QUARTER), jnp.bfloat16)
    high, low = pl.pallas_call(
        functools.partial(table_kernel, hours * hour_parts),
        out_shape=[table_shape] * 2,
        in_specs=[smem],
        out_specs=[vmem] * 2,
        compiler_params=limit,
        cost_estimate=pl.CostEstimate(flops=5_000_000, bytes_accessed=2_000_000, transcendentals=0),
        name="band_table",
    )(pltpu.with_memory_space_constraint(wanted, pltpu.SMEM))

    cross = pl.pallas_call(
        functools.partial(cross_kernel, [*sources, here], parts, freq_parts, stations // SB),
        out_shape=[jax.ShapeDtypeStruct((2, part_pairs, freq_loc), jnp.float32)] * parts,
        in_specs=[smem] + [vmem] * (len(rounds) + 1),
        out_specs=[vmem] * parts,
        scratch_shapes=[
            pltpu.VMEM((2 * reader_blocks, chunks, hours, 2 * SB, LANES), jnp.float32)
        ],
        compiler_params=limit,
        name="cross",
    )(pltpu.with_memory_space_constraint(wanted, pltpu.SMEM), *arrived, own)
    summed = [cross[0]] + [
        exchange(cross[distance], ("hour", "freq"), parts, distance) for distance in range(1, parts)
    ]

    return pl.pallas_call(
        functools.partial(lags_kernel, parts, freq_parts),
        out_shape=jax.ShapeDtypeStruct((part_pairs, L), jnp.float32),
        in_specs=[vmem] * (2 + parts),
        out_specs=vmem,
        compiler_params=limit,
        name="lags",
    )(high, low, *summed)


def solution(mesh):
    sizes = (mesh.shape["stn"], mesh.shape["hour"], mesh.shape["freq"])
    in_specs = (
        P(("groups", "hour"), "stn", None, "freq"),
        P(("groups", "hour"), "stn"),
        P("groups", None),
    )
    out_specs = P(("groups", "stn", "hour", "freq"), None)
    return jax.shard_map(
        functools.partial(per_device, sizes),
        mesh=mesh,
        in_specs=in_specs,
        out_specs=out_specs,
        check_vma=False,
    )
```

```python
import functools
import math

import jax
import jax.numpy as jnp
from jax import lax
from jax.experimental import pallas as pl
from jax.experimental.pallas import tpu as pltpu
from jax.sharding import PartitionSpec as P

L = 1024
SB = 8
CAP = 2
LANES = 128
QUARTER = L // 4


def station_rounds(readers):
    ring = [i // 2 if i % 2 == 0 else readers - 1 - i // 2 for i in range(readers)]
    shifts = [*range(1, readers, 2), *range(2, readers, 2)]
    return [[ring[(ring.index(s) + d) % readers] for s in range(readers)] for d in shifts]


def pick(table, index):
    value = jnp.int32(table[0])
    for position, entry in enumerate(table):
        value = jnp.where(index == position, jnp.int32(entry), value)
    return value


def exchange(x, axes, size, distance):
    return lax.ppermute(x, axes, [(i, i ^ distance) for i in range(size)])


def wanted_slots(pairs_ref, reader, me, reader_blocks, owned):
    starts = [jnp.int32(0)] * CAP
    found = jnp.int32(0)
    for entry in range(2 * reader_blocks):
        block = pairs_ref[entry % 2, reader * reader_blocks + entry // 2]
        mine = (block >= me * owned) & (block < (me + 1) * owned)
        for slot in range(CAP):
            starts[slot] = jnp.where(mine & (found == slot), (block - me * owned) * SB, starts[slot])
        found = found + mine.astype(jnp.int32)
    return starts


def recorded_rows(start, up):
    rows = 2 * SB
    station = lax.broadcasted_iota(jnp.int32, (rows, up.shape[1]), 1)
    row = lax.broadcasted_iota(jnp.int32, (rows, up.shape[1]), 0)
    pick = (station == start + row // 2).astype(jnp.float32).astype(jnp.bfloat16)
    return lax.dot_general(
        pick, up, (((1,), (1,)), ((), ())), preferred_element_type=jnp.float32
    )


def masked_rows(spectra_ref, hour, start, recorded):
    values = spectra_ref[hour, pl.ds(start, SB)].astype(jnp.float32)
    values = values.reshape(2 * SB, spectra_ref.shape[3])
    keep = jnp.broadcast_to(recorded[:, hour : hour + 1], values.shape) > 0
    return jnp.where(keep, values, 0.0).astype(jnp.bfloat16)


def send_kernel(readers, rounds, pairs_hbm, uptime_hbm, spectra_hbm, *refs):
    slot_refs, (pairs_ref, uptime_ref, spectra_ref, sems) = refs[:-4], refs[-4:]
    me = lax.axis_index("stn")
    hours, stations = uptime_ref.shape
    reader_blocks = pairs_ref.shape[1] // readers
    arguments = [
        pltpu.make_async_copy(pairs_hbm, pairs_ref, sems.at[0]),
        pltpu.make_async_copy(uptime_hbm, uptime_ref, sems.at[1]),
    ]
    pieces = 2 if hours % 2 == 0 else 1
    count = hours // pieces
    spectra = []
    for piece in range(pieces):
        some = pl.ds(piece * count, count)
        spectra.append(
            pltpu.make_async_copy(spectra_hbm.at[some], spectra_ref.at[some], sems.at[2 + piece])
        )
    for copy in arguments + spectra:
        copy.start()
    for copy in arguments:
        copy.wait()
    up = uptime_ref[...].astype(jnp.float32).astype(jnp.bfloat16)
    wanted = []
    for slot_ref, targets in zip(slot_refs, rounds, strict=True):
        reader = pick(targets, me)
        starts = wanted_slots(pairs_ref, reader, me, reader_blocks, stations // SB)
        for slot, start in enumerate(starts):
            wanted.append((slot_ref, slot, start, recorded_rows(start, up)))
    for hour in range(hours):
        if hour % count == 0:
            spectra[hour // count].wait()
        for slot_ref, slot, start, recorded in wanted:
            slot_ref[slot, hour] = masked_rows(spectra_ref, hour, start, recorded)


def table_kernel(hour_total, wanted_ref, high_ref, low_ref):
    del wanted_ref
    _, rows, lags = high_ref.shape
    half = L // 2
    tall = 16
    groups = half // tall
    sub = lax.broadcasted_iota(jnp.int32, (tall, LANES), 0)
    lane = lax.broadcasted_iota(jnp.int32, (tall, LANES), 1)
    base_cos, base_sin = circle(sub * lane, L)
    group_cos, group_sin = circle(
        lax.broadcasted_iota(jnp.int32, (groups, LANES), 0)
        * lax.broadcasted_iota(jnp.int32, (groups, LANES), 1),
        L // tall,
    )
    steps = [circle(sub * j, L // LANES) for j in range(1, lags // LANES)]
    weight_cos, weight_sin = circle(2 * sub + 1, 2 * L)
    scale = 1.0 / math.sqrt(hour_total * half)
    for group in range(groups):
        turn_cos, turn_sin = group_cos[group : group + 1], group_sin[group : group + 1]
        quarter_turns = math.pi * tall * group / half
        weight = weight_sin * math.cos(quarter_turns) + weight_cos * math.sin(quarter_turns)
        weight = weight * weight * scale
        cos0 = (base_cos * turn_cos - base_sin * turn_sin) * weight
        sin0 = (base_sin * turn_cos + base_cos * turn_sin) * weight
        chunk, row = divmod(group * tall, LANES)
        at, chunk = divmod(chunk * 2 * LANES, rows)
        for j in range(lags // LANES):
            real, imag = cos0, -sin0
            if j > 0:
                cj, sj = steps[j - 1]
                real, imag = cos0 * cj - sin0 * sj, -(sin0 * cj + cos0 * sj)
            for first, value in ((chunk + row, real), (chunk + LANES + row, imag)):
                where = (at, pl.ds(first, tall), pl.ds(j * LANES, LANES))
                high = value.astype(jnp.bfloat16)
                high_ref[where] = high
                low_ref[where] = (value - high.astype(jnp.float32)).astype(jnp.bfloat16)


def circle(step, steps):
    quarter = steps // 4
    step = step % steps
    turn = (step + quarter // 2) // quarter
    x = (step - turn * quarter).astype(jnp.float32) * (2.0 * math.pi / steps)
    y = x * x
    sin = x * (1.0 + y * (-1 / 6 + y * (1 / 120 + y * (-1 / 5040 + y * (1 / 362880)))))
    cos = 1.0 + y * (-1 / 2 + y * (1 / 24 + y * (-1 / 720 + y * (1 / 40320 - y * (1 / 3628800)))))
    turn = turn % 4
    odd = turn % 2 == 1
    out_cos, out_sin = jnp.where(odd, sin, cos), jnp.where(odd, cos, sin)
    out_cos = jnp.where((turn == 1) | (turn == 2), -out_cos, out_cos)
    out_sin = jnp.where((turn == 2) | (turn == 3), -out_sin, out_sin)
    return out_cos, out_sin


def cross_kernel(rounds, parts, freq_parts, owned, pairs_ref, *refs):
    readers = len(rounds[0])
    count = len(rounds)
    slot_refs, out_refs, blocks = refs[:count], refs[count : count + parts], refs[-1]
    me = lax.axis_index("stn")
    mine = lax.axis_index("hour") * freq_parts + lax.axis_index("freq")
    reader_blocks = pairs_ref.shape[1] // readers
    _, chunks, hours, _, _ = blocks.shape
    wanted = []
    for entry in range(2 * reader_blocks):
        wanted.append(pairs_ref[entry % 2, me * reader_blocks + entry // 2])
    owners = [block // owned for block in wanted]
    for entry in range(2 * reader_blocks):
        slot = jnp.int32(0)
        for before in range(entry):
            slot = slot + (owners[before] == owners[entry]).astype(jnp.int32)
        slot = jnp.minimum(slot, CAP - 1)
        for slot_ref, sources in zip(slot_refs, rounds, strict=True):

            @pl.when(owners[entry] == pick(sources, me))
            def _(entry=entry, slot=slot, slot_ref=slot_ref):
                values = slot_ref[slot].astype(jnp.float32)
                for chunk in range(chunks):
                    blocks[entry, chunk] = values[:, :, chunk * LANES : (chunk + 1) * LANES]

    part_rows = out_refs[0].shape[1] // SB
    for distance in range(parts):
        first_row = (mine ^ distance) * part_rows
        pair = first_row // SB
        station = first_row % SB
        for chunk in range(chunks):
            lanes = pl.ds(chunk * LANES, LANES)
            second = 2 * pair + 1
            second_re = [blocks[second, chunk, h, pl.ds(0, SB, stride=2)] for h in range(hours)]
            second_im = [blocks[second, chunk, h, pl.ds(1, SB, stride=2)] for h in range(hours)]
            for s in range(part_rows):
                real = jnp.zeros((SB, LANES), jnp.float32)
                imag = jnp.zeros((SB, LANES), jnp.float32)
                for h in range(hours):
                    first_re = blocks[2 * pair, chunk, h, pl.ds(2 * (station + s), 1)]
                    first_im = blocks[2 * pair, chunk, h, pl.ds(2 * (station + s) + 1, 1)]
                    real = real + first_re * second_re[h] + first_im * second_im[h]
                    imag = imag + first_im * second_re[h] - first_re * second_im[h]
                out_refs[distance][0, pl.ds(s * SB, SB), lanes] = real
                out_refs[distance][1, pl.ds(s * SB, SB), lanes] = imag


def lags_kernel(c, count, high_ref, low_ref, *refs):
    part_refs, before_refs, out_ref = refs[:count], refs[count:-1], refs[-1]
    table = lax.axis_index("freq") ^ c
    _, pairs, freq_loc = part_refs[0].shape
    phase = lax.broadcasted_iota(jnp.int32, (pairs, LANES), 1) % 4
    highs, lows = [], []
    for first in range(0, freq_loc, LANES):
        lanes = pl.ds(first, LANES)
        cross = part_refs[0][:, :, lanes]
        for part_ref in part_refs[1:]:
            cross = cross + part_ref[:, :, lanes]
        real, imag = cross[0], cross[1]
        turned = []
        for q in range(4):
            step = (phase * q) % 4
            re = jnp.where(step % 2 == 0, real, imag)
            im = jnp.where(step % 2 == 0, imag, real)
            re = jnp.where((step == 1) | (step == 2), -re, re)
            im = jnp.where((step == 2) | (step == 3), -im, im)
            turned.append(jnp.concatenate([re, im], axis=1))
        turned = jnp.concatenate(turned, axis=0)
        high = turned.astype(jnp.bfloat16)
        highs.append(high)
        lows.append((turned - high.astype(jnp.float32)).astype(jnp.bfloat16))
    high, low = jnp.concatenate(highs, axis=1), jnp.concatenate(lows, axis=1)
    both = jnp.concatenate([high, low], axis=0)
    by_high = jnp.dot(both, high_ref[table], preferred_element_type=jnp.float32)
    by_low = jnp.dot(high, low_ref[table], preferred_element_type=jnp.float32)
    total = by_high[: 4 * pairs] + (by_high[4 * pairs :] + by_low)
    for before_ref in before_refs:
        total = total + before_ref[...]
    if out_ref.shape == total.shape:
        out_ref[...] = total
    else:
        for q in range(4):
            out_ref[:, q * QUARTER : (q + 1) * QUARTER] = total[q * pairs : (q + 1) * pairs]


def per_device(sizes, spectra, uptime, pair_blocks):
    readers, hour_parts, freq_parts = sizes
    hours, stations, _, freq_loc = spectra.shape
    parts = hour_parts * freq_parts
    chunks = freq_loc // LANES
    reader_blocks = pair_blocks.shape[0] // readers
    part_pairs = reader_blocks * SB * SB // parts
    pairs = pair_blocks.T
    vmem = pl.BlockSpec(memory_space=pltpu.VMEM)
    smem = pl.BlockSpec(memory_space=pltpu.SMEM)
    hbm = pl.BlockSpec(memory_space=pltpu.HBM)
    limit = pltpu.CompilerParams(vmem_limit_bytes=32 * 1024 * 1024)
    slots_shape = jax.ShapeDtypeStruct((CAP, hours, 2 * SB, freq_loc), jnp.bfloat16)

    rounds = station_rounds(readers)
    here = [*range(readers)]
    *sent, own, wanted = pl.pallas_call(
        functools.partial(send_kernel, readers, [*rounds, here]),
        out_shape=[slots_shape] * (len(rounds) + 1) + [pltpu.SMEM(pairs.shape, jnp.int32)],
        in_specs=[hbm] * 3,
        out_specs=[vmem] * (len(rounds) + 1) + [smem],
        scratch_shapes=[
            pltpu.VMEM(uptime.shape, jnp.int32),
            pltpu.VMEM(spectra.shape, jnp.bfloat16),
            pltpu.SemaphoreType.DMA((4,)),
        ],
        compiler_params=limit,
        name="send_slots",
    )(*[pltpu.with_memory_space_constraint(x, pltpu.HBM) for x in (pairs, uptime, spectra)])
    arrived = [
        lax.ppermute(slots, "stn", [*enumerate(targets)])
        for slots, targets in zip(sent, rounds, strict=True)
    ]
    sources = [[targets.index(t) for t in range(readers)] for targets in rounds]

    table_shape = jax.ShapeDtypeStruct((freq_parts, 2 * freq_loc, QUARTER), jnp.bfloat16)
    high, low = pl.pallas_call(
        functools.partial(table_kernel, hours * hour_parts),
        out_shape=[table_shape] * 2,
        in_specs=[smem],
        out_specs=[vmem] * 2,
        compiler_params=limit,
        cost_estimate=pl.CostEstimate(flops=5_000_000, bytes_accessed=2_000_000, transcendentals=0),
        name="band_table",
    )(pltpu.with_memory_space_constraint(wanted, pltpu.SMEM))

    cross = pl.pallas_call(
        functools.partial(cross_kernel, [*sources, here], parts, freq_parts, stations // SB),
        out_shape=[jax.ShapeDtypeStruct((2, part_pairs, freq_loc), jnp.float32)] * parts,
        in_specs=[smem] + [vmem] * (len(rounds) + 1),
        out_specs=[vmem] * parts,
        scratch_shapes=[
            pltpu.VMEM((2 * reader_blocks, chunks, hours, 2 * SB, LANES), jnp.float32)
        ],
        compiler_params=limit,
        name="cross",
    )(pltpu.with_memory_space_constraint(wanted, pltpu.SMEM), *arrived, own)
    summed = [cross[0]] + [
        exchange(cross[distance], ("hour", "freq"), parts, distance) for distance in range(1, parts)
    ]

    lags = []
    for c in range(freq_parts):
        shares = summed[c::freq_parts]
        last = c == freq_parts - 1
        lags = pl.pallas_call(
            functools.partial(lags_kernel, c, len(shares)),
            out_shape=[
                jax.ShapeDtypeStruct((part_pairs, L) if last else (4 * part_pairs, QUARTER), jnp.float32)
            ],
            in_specs=[vmem] * (2 + len(shares) + len(lags)),
            out_specs=[vmem],
            compiler_params=limit,
            name="lags",
        )(high, low, *shares, *lags)
    return lags[0]


def solution(mesh):
    sizes = (mesh.shape["stn"], mesh.shape["hour"], mesh.shape["freq"])
    in_specs = (
        P(("groups", "hour"), "stn", None, "freq"),
        P(("groups", "hour"), "stn"),
        P("groups", None),
    )
    out_specs = P(("groups", "stn", "hour", "freq"), None)
    return jax.shard_map(
        functools.partial(per_device, sizes),
        mesh=mesh,
        in_specs=in_specs,
        out_specs=out_specs,
        check_vma=False,
    )
```

```python
import functools
import math

import jax
import jax.numpy as jnp
from jax import lax
from jax.experimental import pallas as pl
from jax.experimental.pallas import tpu as pltpu
from jax.sharding import PartitionSpec as P

L = 1024
SB = 8
CAP = 2
LANES = 128
QUARTER = L // 4


def station_rounds(readers):
    ring = [i // 2 if i % 2 == 0 else readers - 1 - i // 2 for i in range(readers)]
    shifts = [*range(1, readers, 2), *range(2, readers, 2)]
    return [[ring[(ring.index(s) + d) % readers] for s in range(readers)] for d in shifts]


def pick(table, index):
    value = jnp.int32(table[0])
    for position, entry in enumerate(table):
        value = jnp.where(index == position, jnp.int32(entry), value)
    return value


def exchange(x, axes, size, distance):
    return lax.ppermute(x, axes, [(i, i ^ distance) for i in range(size)])


def wanted_slots(pairs_ref, reader, me, reader_blocks, owned):
    starts = [jnp.int32(0)] * CAP
    found = jnp.int32(0)
    for entry in range(2 * reader_blocks):
        block = pairs_ref[entry % 2, reader * reader_blocks + entry // 2]
        mine = (block >= me * owned) & (block < (me + 1) * owned)
        for slot in range(CAP):
            starts[slot] = jnp.where(mine & (found == slot), (block - me * owned) * SB, starts[slot])
        found = found + mine.astype(jnp.int32)
    return starts


def recorded_rows(start, up):
    rows = 2 * SB
    station = lax.broadcasted_iota(jnp.int32, (rows, up.shape[1]), 1)
    row = lax.broadcasted_iota(jnp.int32, (rows, up.shape[1]), 0)
    pick = (station == start + row // 2).astype(jnp.float32).astype(jnp.bfloat16)
    return lax.dot_general(
        pick, up, (((1,), (1,)), ((), ())), preferred_element_type=jnp.float32
    )


def masked_rows(spectra_ref, hour, start, recorded):
    values = spectra_ref[hour, pl.ds(start, SB)].astype(jnp.float32)
    values = values.reshape(2 * SB, spectra_ref.shape[3])
    keep = jnp.broadcast_to(recorded[:, hour : hour + 1], values.shape) > 0
    return jnp.where(keep, values, 0.0).astype(jnp.bfloat16)


def send_kernel(readers, rounds, pairs_hbm, uptime_hbm, spectra_hbm, *refs):
    slot_refs, (pairs_ref, uptime_ref, spectra_ref, sems) = refs[:-4], refs[-4:]
    me = lax.axis_index("stn")
    hours, stations = uptime_ref.shape
    reader_blocks = pairs_ref.shape[1] // readers
    arguments = [
        pltpu.make_async_copy(pairs_hbm, pairs_ref, sems.at[0]),
        pltpu.make_async_copy(uptime_hbm, uptime_ref, sems.at[1]),
    ]
    pieces = 2 if hours % 2 == 0 else 1
    count = hours // pieces
    spectra = []
    for piece in range(pieces):
        some = pl.ds(piece * count, count)
        spectra.append(
            pltpu.make_async_copy(spectra_hbm.at[some], spectra_ref.at[some], sems.at[2 + piece])
        )
    for copy in arguments + spectra:
        copy.start()
    for copy in arguments:
        copy.wait()
    up = uptime_ref[...].astype(jnp.float32).astype(jnp.bfloat16)
    wanted = []
    for slot_ref, targets in zip(slot_refs, rounds, strict=True):
        reader = pick(targets, me)
        starts = wanted_slots(pairs_ref, reader, me, reader_blocks, stations // SB)
        for slot, start in enumerate(starts):
            wanted.append((slot_ref, slot, start, recorded_rows(start, up)))
    for hour in range(hours):
        if hour % count == 0:
            spectra[hour // count].wait()
        for slot_ref, slot, start, recorded in wanted:
            slot_ref[slot, hour] = masked_rows(spectra_ref, hour, start, recorded)


def table_kernel(hour_total, wanted_ref, high_ref, low_ref):
    del wanted_ref
    _, rows, lags = high_ref.shape
    half = L // 2
    tall = 16
    groups = half // tall
    sub = lax.broadcasted_iota(jnp.int32, (tall, LANES), 0)
    lane = lax.broadcasted_iota(jnp.int32, (tall, LANES), 1)
    base_cos, base_sin = circle(sub * lane, L)
    group_cos, group_sin = circle(
        lax.broadcasted_iota(jnp.int32, (groups, LANES), 0)
        * lax.broadcasted_iota(jnp.int32, (groups, LANES), 1),
        L // tall,
    )
    steps = [circle(sub * j, L // LANES) for j in range(1, lags // LANES)]
    weight_cos, weight_sin = circle(2 * sub + 1, 2 * L)
    scale = 1.0 / math.sqrt(hour_total * half)
    for group in range(groups):
        turn_cos, turn_sin = group_cos[group : group + 1], group_sin[group : group + 1]
        quarter_turns = math.pi * tall * group / half
        weight = weight_sin * math.cos(quarter_turns) + weight_cos * math.sin(quarter_turns)
        weight = weight * weight * scale
        cos0 = (base_cos * turn_cos - base_sin * turn_sin) * weight
        sin0 = (base_sin * turn_cos + base_cos * turn_sin) * weight
        chunk, row = divmod(group * tall, LANES)
        at, chunk = divmod(chunk * 2 * LANES, rows)
        for j in range(lags // LANES):
            real, imag = cos0, -sin0
            if j > 0:
                cj, sj = steps[j - 1]
                real, imag = cos0 * cj - sin0 * sj, -(sin0 * cj + cos0 * sj)
            for first, value in ((chunk + row, real), (chunk + LANES + row, imag)):
                where = (at, pl.ds(first, tall), pl.ds(j * LANES, LANES))
                high = value.astype(jnp.bfloat16)
                high_ref[where] = high
                low_ref[where] = (value - high.astype(jnp.float32)).astype(jnp.bfloat16)


def circle(step, steps):
    quarter = steps // 4
    step = step % steps
    turn = (step + quarter // 2) // quarter
    x = (step - turn * quarter).astype(jnp.float32) * (2.0 * math.pi / steps)
    y = x * x
    sin = x * (1.0 + y * (-1 / 6 + y * (1 / 120 + y * (-1 / 5040 + y * (1 / 362880)))))
    cos = 1.0 + y * (-1 / 2 + y * (1 / 24 + y * (-1 / 720 + y * (1 / 40320 - y * (1 / 3628800)))))
    turn = turn % 4
    odd = turn % 2 == 1
    out_cos, out_sin = jnp.where(odd, sin, cos), jnp.where(odd, cos, sin)
    out_cos = jnp.where((turn == 1) | (turn == 2), -out_cos, out_cos)
    out_sin = jnp.where((turn == 2) | (turn == 3), -out_sin, out_sin)
    return out_cos, out_sin


def cross_kernel(rounds, targets, freq_parts, owned, pairs_ref, *refs):
    readers = len(rounds[0])
    count = len(rounds)
    slot_refs, out_refs, blocks = refs[:count], refs[count:-1], refs[-1]
    me = lax.axis_index("stn")
    mine = lax.axis_index("hour") * freq_parts + lax.axis_index("freq")
    reader_blocks = pairs_ref.shape[1] // readers
    _, chunks, hours, _, _ = blocks.shape
    wanted = []
    for entry in range(2 * reader_blocks):
        wanted.append(pairs_ref[entry % 2, me * reader_blocks + entry // 2])
    owners = [block // owned for block in wanted]
    part_rows = out_refs[0].shape[1] // SB
    first_rows = [(mine ^ distance) * part_rows for distance in targets]
    for entry in range(2 * reader_blocks):
        slot = jnp.int32(0)
        for before in range(entry):
            slot = slot + (owners[before] == owners[entry]).astype(jnp.int32)
        slot = jnp.minimum(slot, CAP - 1)
        needed = first_rows[0] // SB == entry // 2
        for first_row in first_rows[1:]:
            needed = needed | (first_row // SB == entry // 2)
        for slot_ref, sources in zip(slot_refs, rounds, strict=True):

            @pl.when(needed & (owners[entry] == pick(sources, me)))
            def _(entry=entry, slot=slot, slot_ref=slot_ref):
                values = slot_ref[slot].astype(jnp.float32)
                for chunk in range(chunks):
                    blocks[entry, chunk] = values[:, :, chunk * LANES : (chunk + 1) * LANES]

    for out_ref, first_row in zip(out_refs, first_rows, strict=True):
        pair = first_row // SB
        station = first_row % SB
        for chunk in range(chunks):
            lanes = pl.ds(chunk * LANES, LANES)
            second = 2 * pair + 1
            second_re = [blocks[second, chunk, h, pl.ds(0, SB, stride=2)] for h in range(hours)]
            second_im = [blocks[second, chunk, h, pl.ds(1, SB, stride=2)] for h in range(hours)]
            for s in range(part_rows):
                real = jnp.zeros((SB, LANES), jnp.float32)
                imag = jnp.zeros((SB, LANES), jnp.float32)
                for h in range(hours):
                    first_re = blocks[2 * pair, chunk, h, pl.ds(2 * (station + s), 1)]
                    first_im = blocks[2 * pair, chunk, h, pl.ds(2 * (station + s) + 1, 1)]
                    real = real + first_re * second_re[h] + first_im * second_im[h]
                    imag = imag + first_im * second_re[h] - first_re * second_im[h]
                out_ref[0, pl.ds(s * SB, SB), lanes] = real
                out_ref[1, pl.ds(s * SB, SB), lanes] = imag


def lags_kernel(c, count, high_ref, low_ref, *refs):
    part_refs, before_refs, out_ref = refs[:count], refs[count:-1], refs[-1]
    table = lax.axis_index("freq") ^ c
    _, pairs, freq_loc = part_refs[0].shape
    phase = lax.broadcasted_iota(jnp.int32, (pairs, LANES), 1) % 4
    highs, lows = [], []
    for first in range(0, freq_loc, LANES):
        lanes = pl.ds(first, LANES)
        cross = part_refs[0][:, :, lanes]
        for part_ref in part_refs[1:]:
            cross = cross + part_ref[:, :, lanes]
        real, imag = cross[0], cross[1]
        turned = []
        for q in range(4):
            step = (phase * q) % 4
            re = jnp.where(step % 2 == 0, real, imag)
            im = jnp.where(step % 2 == 0, imag, real)
            re = jnp.where((step == 1) | (step == 2), -re, re)
            im = jnp.where((step == 2) | (step == 3), -im, im)
            turned.append(jnp.concatenate([re, im], axis=1))
        turned = jnp.concatenate(turned, axis=0)
        high = turned.astype(jnp.bfloat16)
        highs.append(high)
        lows.append((turned - high.astype(jnp.float32)).astype(jnp.bfloat16))
    high, low = jnp.concatenate(highs, axis=1), jnp.concatenate(lows, axis=1)
    both = jnp.concatenate([high, low], axis=0)
    by_high = jnp.dot(both, high_ref[table], preferred_element_type=jnp.float32)
    by_low = jnp.dot(high, low_ref[table], preferred_element_type=jnp.float32)
    total = by_high[: 4 * pairs] + (by_high[4 * pairs :] + by_low)
    for before_ref in before_refs:
        total = total + before_ref[...]
    if out_ref.shape == total.shape:
        out_ref[...] = total
    else:
        for q in range(4):
            out_ref[:, q * QUARTER : (q + 1) * QUARTER] = total[q * pairs : (q + 1) * pairs]


def per_device(sizes, spectra, uptime, pair_blocks):
    readers, hour_parts, freq_parts = sizes
    hours, stations, _, freq_loc = spectra.shape
    parts = hour_parts * freq_parts
    chunks = freq_loc // LANES
    reader_blocks = pair_blocks.shape[0] // readers
    part_pairs = reader_blocks * SB * SB // parts
    pairs = pair_blocks.T
    vmem = pl.BlockSpec(memory_space=pltpu.VMEM)
    smem = pl.BlockSpec(memory_space=pltpu.SMEM)
    hbm = pl.BlockSpec(memory_space=pltpu.HBM)
    limit = pltpu.CompilerParams(vmem_limit_bytes=32 * 1024 * 1024)
    slots_shape = jax.ShapeDtypeStruct((CAP, hours, 2 * SB, freq_loc), jnp.bfloat16)

    rounds = station_rounds(readers)
    here = [*range(readers)]
    *sent, own, wanted = pl.pallas_call(
        functools.partial(send_kernel, readers, [*rounds, here]),
        out_shape=[slots_shape] * (len(rounds) + 1) + [pltpu.SMEM(pairs.shape, jnp.int32)],
        in_specs=[hbm] * 3,
        out_specs=[vmem] * (len(rounds) + 1) + [smem],
        scratch_shapes=[
            pltpu.VMEM(uptime.shape, jnp.int32),
            pltpu.VMEM(spectra.shape, jnp.bfloat16),
            pltpu.SemaphoreType.DMA((4,)),
        ],
        compiler_params=limit,
        name="send_slots",
    )(*[pltpu.with_memory_space_constraint(x, pltpu.HBM) for x in (pairs, uptime, spectra)])
    arrived = [
        lax.ppermute(slots, "stn", [*enumerate(targets)])
        for slots, targets in zip(sent, rounds, strict=True)
    ]
    sources = [[targets.index(t) for t in range(readers)] for targets in rounds]

    table_shape = jax.ShapeDtypeStruct((freq_parts, 2 * freq_loc, QUARTER), jnp.bfloat16)
    high, low = pl.pallas_call(
        functools.partial(table_kernel, hours * hour_parts),
        out_shape=[table_shape] * 2,
        in_specs=[smem],
        out_specs=[vmem] * 2,
        compiler_params=limit,
        cost_estimate=pl.CostEstimate(flops=5_000_000, bytes_accessed=2_000_000, transcendentals=0),
        name="band_table",
    )(pltpu.with_memory_space_constraint(wanted, pltpu.SMEM))

    summed = [None] * parts
    for targets in ([*range(1, parts)], [0]):
        cross = pl.pallas_call(
            functools.partial(cross_kernel, [*sources, here], targets, freq_parts, stations // SB),
            out_shape=[jax.ShapeDtypeStruct((2, part_pairs, freq_loc), jnp.float32)] * len(targets),
            in_specs=[smem] + [vmem] * (len(rounds) + 1),
            out_specs=[vmem] * len(targets),
            scratch_shapes=[
                pltpu.VMEM((2 * reader_blocks, chunks, hours, 2 * SB, LANES), jnp.float32)
            ],
            compiler_params=limit,
            name="cross",
        )(pltpu.with_memory_space_constraint(wanted, pltpu.SMEM), *arrived, own)
        for part, distance in zip(cross, targets, strict=True):
            summed[distance] = (
                exchange(part, ("hour", "freq"), parts, distance) if distance else part
            )

    lags = []
    for c in range(freq_parts):
        shares = summed[c::freq_parts]
        last = c == freq_parts - 1
        lags = pl.pallas_call(
            functools.partial(lags_kernel, c, len(shares)),
            out_shape=[
                jax.ShapeDtypeStruct((part_pairs, L) if last else (4 * part_pairs, QUARTER), jnp.float32)
            ],
            in_specs=[vmem] * (2 + len(shares) + len(lags)),
            out_specs=[vmem],
            compiler_params=limit,
            name="lags",
        )(high, low, *shares, *lags)
    return lags[0]


def solution(mesh):
    sizes = (mesh.shape["stn"], mesh.shape["hour"], mesh.shape["freq"])
    in_specs = (
        P(("groups", "hour"), "stn", None, "freq"),
        P(("groups", "hour"), "stn"),
        P("groups", None),
    )
    out_specs = P(("groups", "stn", "hour", "freq"), None)
    return jax.shard_map(
        functools.partial(per_device, sizes),
        mesh=mesh,
        in_specs=in_specs,
        out_specs=out_specs,
        check_vma=False,
    )
```
